32 devices in a mesh: groups: 2 (over y), tile: 4 (over z), inst: 4 (over x, core).
Axes of the slice: x: 2, y: 2, z: 4, core: 2. Of those that a mesh axis runs over, the one named last changes fastest.
Arguments:
- features: bfloat16 [512, 256, 256], P(('groups', 'tile')), parts along dimension 0, may hold values from -6 to 6
- kernels: bfloat16 [2048, 256], P(('groups', 'tile', 'inst')), parts along dimension 0, may hold values from -0.375 to 0.375
- home: int32 [2048, 1], P(('groups', 'tile', 'inst')), parts along dimension 0, may hold values from 0 to 3; in each aligned block of 64 rows (0 to 63, 64 to 127, ...) at most 40 rows name the same one
- boxes: int32 [2048, 4], P(('groups', 'tile', 'inst')), parts along dimension 0, may hold values from 0 to 7, as said below
- gain: float32 [256], replicated, may hold values from 0.1 to 1.9
- w_in: bfloat16 [256, 2048], P(None, 'inst'), may hold values from -0.375 to 0.375
- w_out: bfloat16 [2048, 256], P('inst'), may hold values from -0.125 to 0.125
Outputs:
- updated: bfloat16 [2048, 256], P(('groups', 'tile', 'inst')), parts along dimension 0
The draws below stay inside these ranges and needn't reach their ends.
There are 2 independent parts, one for each index of `groups`. The reference program is written for one: setup_inputs(seed, part) draws one part's arguments, and reference() takes and returns one part's arrays. A program takes and returns all parts, laid end to end along the dimension named above; an argument that names none is the same for every part. Nothing has to cross between parts.
Inputs may be any that keep to these rules, and one draw needn't show every extreme that they name: `home`: each device's 64 rows name any one strip at most 40 times, and in some of these aligned blocks one strip is named exactly 40 times. `boxes`: each row holds first row <= last row of tiles, both below 2, then first column <= last column, both below 8.
All inputs are finite; a program needn't handle non-finite values.
Results may differ from the reference program's by a relative error of at most 0.0058.
Values may be sent and summed in bfloat16 or wider, within the bound.
No kernel may reach another device: no remote copies, remote signals or barrier semaphores. Data moves between devices by JAX's collectives and lax.ppermute only.
A program may use at most 64 MiB of HBM per device.

```python
import math
import jax
import jax.numpy as jnp
import numpy as np
from jax import lax

C = 256
HID = 2048
TS = 32
SR = 2
WC = 8
KD = 64
CAP = 40
NK = 1024
H = 256
W = 256
N_TILE = 4
N_INST = 4


def draw_boxes(key, part):
    key = jax.random.fold_in(key, 7)
    keys = jax.random.split(key, 4)
    row_one = jax.random.randint(keys[0], (NK,), 0, SR)
    row_two = jax.random.randint(keys[1], (NK,), 0, SR)
    col_one = jax.random.randint(keys[2], (NK,), 0, WC)
    col_two = jax.random.randint(keys[3], (NK,), 0, WC)
    stacked = jnp.stack([jnp.minimum(row_one, row_two), jnp.maximum(row_one, row_two), jnp.minimum(col_one, col_two), jnp.maximum(col_one, col_two)], axis=1)
    return stacked.astype(jnp.int32)


def levels(rng, extent, cuts, least, top_value):
    loudness, own = 1.0, jax.random.fold_in(rng, 6)
    for axis_at, parts in cuts:
        draws = jnp.exp(jax.random.uniform(jax.random.fold_in(own, axis_at), (parts,), jnp.float32, least / len(cuts), top_value / len(cuts)))
        loudness = loudness * jnp.repeat(draws, extent[axis_at] // parts).reshape([-1 if axis == axis_at else 1 for axis in range(len(extent))])
    return loudness


def assign_block(rng, own, number, rows, number_of, top, most, lean):
    sequence = jax.random.permutation(rng, number_of)
    crowded, common = portions_of(number_of, rows * top, most, lean, True), portions_of(number_of, rows * top, most, lean, False)
    places = jnp.arange(number_of)

    def named(tallies, turn):
        used = int((tallies > 0).sum())
        fixed = max(1, used // 4)
        shifted = fixed + (places - fixed + turn * (used - fixed)) % max(1, number_of - fixed)
        return jnp.zeros((number_of,), jnp.int32).at[sequence[jnp.where(places < fixed, places, shifted)]].set(jnp.asarray(tallies, jnp.int32))

    tallies = jnp.where(number % 4 == 0, named(crowded, number // 4), named(common, number - number // 4 - 1))
    mixed = jax.random.permutation(jax.random.fold_in(own, 3), number_of)
    donor, sink = mixed[0:number_of // 2 * 2:2], mixed[1:number_of // 2 * 2:2]
    slack = jnp.minimum(tallies[donor] - 1, most - tallies[sink]) // 2
    slack = jnp.where((donor == sequence[0]) | (sink == sequence[0]) | (tallies[sink] == 0), 0, jnp.maximum(slack, 0))
    shifted = jax.random.randint(jax.random.fold_in(own, 4), (number_of // 2,), 0, 1 << 20) % (slack + 1)
    tallies = tallies.at[donor].add(-shifted).at[sink].add(shifted)
    labels = jnp.searchsorted(jnp.cumsum(tallies), jnp.arange(rows * top), side="right").astype(jnp.int32)
    table = labels.reshape(top, rows).T
    table = table[jax.random.permutation(jax.random.fold_in(own, 1), rows)]
    turn = jax.random.randint(jax.random.fold_in(own, 2), (rows, 1), 0, top)
    return jnp.take_along_axis(table, (jnp.arange(top)[None, :] + turn) % top, axis=1)


def portions_of(amount, total, limit, skew, full):
    loads = [(1 << 20) // math.isqrt(rank ** skew) + 1 for rank in range(1, amount + 1)]
    largest = limit if full else min(limit, max(-(-total // amount), total * loads[0] // sum(loads)))
    least = 1 if total - largest >= amount - 1 else 0
    holding, surplus = [largest] + [least] * (amount - 1), total - largest - least * (amount - 1)
    while surplus > 0:
        movable = [i for i in range(1, amount) if holding[i] < largest] or [i for i in range(1, amount) if holding[i] < limit]
        whole, budget = sum([loads[i] for i in movable]), surplus
        for i in movable:
            more = min(limit - holding[i], max(1, budget * loads[i] // whole), surplus)
            holding[i] = holding[i] + more
            surplus = surplus - more
    return np.array(holding)


def normal_values(stream_key, dims, width, limit, pieces=(), kind=jnp.bfloat16):
    level = levels(stream_key, dims, pieces, -0.22, 0.18) if pieces else 1.0
    result = jax.random.normal(stream_key, dims, jnp.float32) * width * level
    return jnp.minimum(jnp.maximum(result, -limit), limit).astype(kind)


def setup_inputs(seed: int = 0, part: int = 0) -> dict:
    streams_of = jax.random.split(jax.random.key(seed), 8)
    part_keys = jax.random.split(jax.random.fold_in(streams_of[7], part), 8)
    features = normal_values(part_keys[0], (H, W, C), 1.0, 6.0, ((0, 4),))
    kernels = normal_values(part_keys[1], (NK, C), C ** -0.5, 0.375, ((0, 16),))
    home_keys = jax.random.split(jax.random.fold_in(part_keys[2], 1), NK // KD)
    home_turns = jax.random.permutation(jax.random.fold_in(part_keys[2], 3), NK // KD)
    home = jax.vmap(lambda own, number: assign_block(jax.random.fold_in(part_keys[2], 2), own, number, KD, N_TILE, 1, CAP, 2))(home_keys, home_turns).reshape((NK, 1))
    boxes = draw_boxes(jax.random.fold_in(jax.random.fold_in(streams_of[7], part), 71), part)
    gain = jnp.clip(1.0 + 0.18 * jax.random.normal(streams_of[4], (C,), jnp.float32), 0.1, 1.9)
    w_in = normal_values(streams_of[5], (C, HID), C ** -0.5, 0.375, ((1, 4),))
    w_out = normal_values(streams_of[6], (HID, C), HID ** -0.5, 0.125, ((0, 4),))
    return {"features": features, "kernels": kernels, "home": home, "boxes": boxes, "gain": gain, "w_in": w_in, "w_out": w_out}


def tile_pool(kernel_rows, box_rows, strip_feats):
    pooled = jnp.zeros((kernel_rows.shape[0], kernel_rows.shape[1]), jnp.float32)
    covered = jnp.zeros((kernel_rows.shape[0],), jnp.float32)
    for tile_row in range(SR):
        for tile_col in range(WC):
            block = strip_feats[tile_row * TS:(tile_row + 1) * TS, tile_col * TS:(tile_col + 1) * TS]
            block = block.reshape(TS * TS, kernel_rows.shape[1])
            logits = lax.dot_general(kernel_rows, block, (((1,), (1,)), ((), ())), preferred_element_type=jnp.float32)
            inside = (box_rows[:, 0] <= tile_row) & (tile_row <= box_rows[:, 1]) & (box_rows[:, 2] <= tile_col) & (tile_col <= box_rows[:, 3])
            masked = jnp.where(inside[:, None], jax.nn.sigmoid(logits), jnp.zeros_like(logits)).astype(jnp.bfloat16)
            pooled = pooled + jnp.dot(masked, block, preferred_element_type=jnp.float32)
            covered = covered + lax.optimization_barrier(jnp.sum(masked.astype(jnp.float32), axis=1))
    return (pooled, covered)

def reference(features, kernels, home, boxes, gain, w_in, w_out):
    strip_ids = home[:, 0]
    window = N_TILE * N_INST * CAP
    order_idx = jnp.argsort(strip_ids, stable=True).astype(jnp.int32)
    member = (strip_ids[:, None] == jnp.arange(N_TILE, dtype=jnp.int32)[None, :]).astype(jnp.int32)
    counts = lax.optimization_barrier(jnp.sum(member, axis=0)).astype(jnp.int32)
    offsets = (jnp.cumsum(counts) - counts).astype(jnp.int32)
    sorted_rows = jnp.concatenate([kernels[order_idx], jnp.zeros((window, C), kernels.dtype)], axis=0)
    empty_boxes = jnp.tile(jnp.array([[1, 0, 1, 0]], jnp.int32), (window, 1))
    sorted_boxes = jnp.concatenate([boxes[order_idx], empty_boxes], axis=0)
    sorted_ids = jnp.concatenate([order_idx, jnp.full((window,), NK, jnp.int32)])
    feat_map = features.reshape(N_TILE, SR * TS, WC * TS, C)

    def one_strip(carry, strip_id):
        pooled_all, covered_all = carry
        start_at = offsets[strip_id].astype(jnp.int32)
        kernel_rows = lax.dynamic_slice_in_dim(sorted_rows, start_at, window, 0)
        box_rows = lax.dynamic_slice_in_dim(sorted_boxes, start_at, window, 0)
        row_ids = lax.dynamic_slice_in_dim(sorted_ids, start_at, window, 0)
        is_valid = jnp.arange(window, dtype=jnp.int32) < counts[strip_id]
        targets = jnp.where(is_valid, row_ids, NK).astype(jnp.int32)
        strip_feats = lax.dynamic_index_in_dim(feat_map, strip_id, 0, keepdims=False)
        pooled, covered = tile_pool(kernel_rows, box_rows, strip_feats)
        pooled_all = pooled_all.at[targets].set(pooled, mode='drop')
        covered_all = covered_all.at[targets].set(covered, mode='drop')
        return ((pooled_all, covered_all), None)
    start_state = (jnp.zeros((NK, C), jnp.float32), jnp.ones((NK,), jnp.float32))
    (pooled_all, covered_all), unused = lax.scan(one_strip, start_state, jnp.arange(N_TILE, dtype=jnp.int32))
    merged = kernels.astype(jnp.float32) + pooled_all / covered_all[:, None]
    centred = merged - lax.optimization_barrier(jnp.mean(merged, axis=1, keepdims=True))
    spread = lax.optimization_barrier(jnp.mean(centred * centred, axis=1, keepdims=True))
    normed = (centred * lax.rsqrt(spread + 1e-05) * gain[None, :]).astype(jnp.bfloat16)
    hidden = jax.nn.relu(jnp.dot(normed, w_in, preferred_element_type=jnp.float32)).astype(jnp.bfloat16)
    return (merged + jnp.dot(hidden, w_out, preferred_element_type=jnp.float32)).astype(jnp.bfloat16)
```

```python
import functools

import jax
import jax.numpy as jnp
from jax import lax
from jax.experimental import pallas as pl
from jax.experimental.pallas import tpu as pltpu
from jax.sharding import PartitionSpec as P

TS = 32
SR = 2
WC = 8
META = 16
ROWS_PER_STEP = 4
VMEM = pltpu.VMEM


def pack_kernel(kernels_ref, home_ref, boxes_ref, out_ref):
    count = kernels_ref.shape[0]
    out_ref[:count, :] = kernels_ref[...]
    out_ref[count:, :] = jnp.zeros((META, out_ref.shape[1]), out_ref.dtype)
    line = lax.broadcasted_iota(jnp.int32, (META, count), 0)
    meta = jnp.where(line == 0, home_ref[...], 0)
    for i in range(4):
        meta = jnp.where(line == i + 1, boxes_ref[i : i + 1, :], meta)
    out_ref[count:, :count] = meta.astype(jnp.float32).astype(out_ref.dtype)


def update_kernel(blocks, shards, slots, count, *refs):
    block_refs, refs = refs[:blocks], refs[blocks:]
    features_ref, gain_ref, refs = refs[0], refs[1], refs[2:]
    in_refs, out_w_refs, out_refs = refs[:shards], refs[shards : 2 * shards], refs[2 * shards :]
    bf16, f32 = jnp.bfloat16, jnp.float32
    mine = lax.axis_index("tile")
    stride, feat = count + META, block_refs[0].shape[1]
    sources = [
        (ref, i) for ref in block_refs for i in range(ref.shape[0] // stride)
    ]

    earlier = (
        lax.broadcasted_iota(jnp.int32, (count, count), 0)
        < lax.broadcasted_iota(jnp.int32, (count, count), 1)
    ).astype(bf16)
    slot = lax.broadcasted_iota(jnp.int32, (slots, count), 0).astype(f32)
    base = jnp.zeros((1, 1), f32)
    rows = jnp.zeros((slots, feat), f32)
    bounds = jnp.zeros((slots, META), f32)
    select = []
    for ref, i in sources:
        meta = ref[i * stride + count : (i + 1) * stride, :count]
        member = jnp.where(meta[0:1].astype(f32) == mine.astype(f32), 1.0, 0.0)
        rank = jnp.dot(
            jnp.broadcast_to(member, (8, count)).astype(bf16), earlier, preferred_element_type=f32
        )[0:1]
        pick = jnp.where((rank + base == slot) & (member > 0.0), 1.0, 0.0)
        pick16 = pick.astype(bf16)
        rows = rows + jnp.dot(
            pick16, ref[i * stride : i * stride + count, :], preferred_element_type=f32
        )
        bounds = bounds + lax.dot_general(
            pick16, meta, (((1,), (1,)), ((), ())), preferred_element_type=f32
        )
        select.append(pick.T.astype(bf16))
        base = base + jnp.sum(member, axis=1, keepdims=True)
    rows16 = rows.astype(bf16)

    width = WC * TS
    tile_col = (lax.broadcasted_iota(jnp.int32, (slots, width), 1) // TS).astype(f32)
    column = (bounds[:, 3:4] <= tile_col) & (tile_col <= bounds[:, 4:5])
    inside = [
        jnp.where(column & (bounds[:, 1:2] <= r) & (r <= bounds[:, 2:3]), 1.0, 0.0)
        for r in range(SR)
    ]

    steps = features_ref.shape[0] // ROWS_PER_STEP

    def cells(step):
        return features_ref[step * ROWS_PER_STEP : (step + 1) * ROWS_PER_STEP].reshape(
            ROWS_PER_STEP * width, feat
        )

    def logits(step):
        return lax.dot_general(
            rows16, cells(step), (((1,), (1,)), ((), ())), preferred_element_type=f32
        )

    pooled = jnp.zeros((slots, feat), f32)
    covered = jnp.zeros((slots, width), f32)
    now = logits(0)
    for step in range(steps):
        later = logits(step + 1) if step + 1 < steps else None
        mask = inside[step * ROWS_PER_STEP // TS]
        parts = []
        for j in range(ROWS_PER_STEP):
            part = mask * pl.reciprocal(
                1.0 + jnp.exp(-now[:, j * width : (j + 1) * width]), approx=True
            )
            covered = covered + part
            parts.append(part.astype(bf16))
        pooled = pooled + jnp.dot(
            jnp.concatenate(parts, axis=1), cells(step), preferred_element_type=f32
        )
        now = later
    area = jnp.sum(covered, axis=1, keepdims=True)

    merged = rows + pooled / area
    centred = merged - jnp.mean(merged, axis=1, keepdims=True)
    spread = jnp.mean(centred * centred, axis=1, keepdims=True)
    normed = (centred * lax.rsqrt(spread + 1e-05) * gain_ref[...]).astype(bf16)
    total = merged
    for w_in_ref, w_out_ref in zip(in_refs, out_w_refs):
        hidden = jnp.maximum(jnp.dot(normed, w_in_ref[...], preferred_element_type=f32), 0.0)
        total = total + jnp.dot(hidden.astype(bf16), w_out_ref[...], preferred_element_type=f32)
    updated = total.astype(bf16)

    for k, pick in enumerate(select):
        back = jnp.dot(pick, updated, preferred_element_type=f32).astype(bf16)
        ref, i = out_refs[k * len(out_refs) // len(select)], k % (len(select) // len(out_refs))
        ref[i * count : (i + 1) * count, :] = back


def shifted(x, axis, shift):
    size = lax.axis_size(axis)
    return lax.ppermute(x, axis, [(i, (i + shift) % size) for i in range(size)])


def local(features, kernels, home, boxes, gain, w_in, w_out):
    strips, holders = lax.axis_size("tile"), lax.axis_size("inst")
    count, feat = kernels.shape
    slots = strips * min(count, max(2, 5 * count // (2 * strips)))
    near = strips <= 8

    block = pl.pallas_call(
        pack_kernel,
        out_shape=jax.ShapeDtypeStruct((count + META, feat), kernels.dtype),
        in_specs=[pl.BlockSpec(memory_space=VMEM)] * 3,
        out_specs=pl.BlockSpec(memory_space=VMEM),
        name="pack",
    )(kernels, home.T, boxes.T)
    if near:
        blocks = [block] + [shifted(block, "tile", s) for s in range(1, strips)]
        outs = [jax.ShapeDtypeStruct((count, feat), kernels.dtype)] * strips
    else:
        blocks = [lax.all_gather(block, "tile", axis=0, tiled=True)]
        outs = [jax.ShapeDtypeStruct((strips * count, feat), kernels.dtype)]

    shards_in = [w_in] + [shifted(w_in, "inst", s) for s in range(1, holders)]
    shards_out = [w_out] + [shifted(w_out, "inst", s) for s in range(1, holders)]

    back = pl.pallas_call(
        functools.partial(update_kernel, len(blocks), holders, slots, count),
        out_shape=outs,
        in_specs=[pl.BlockSpec(memory_space=VMEM)] * (len(blocks) + 2 + 2 * holders),
        out_specs=[pl.BlockSpec(memory_space=VMEM)] * len(outs),
        compiler_params=pltpu.CompilerParams(vmem_limit_bytes=40 << 20),
        name="update",
    )(*blocks, features, gain.reshape(1, feat), *shards_in, *shards_out)
    if near:
        mine = back[0]
        for s in range(1, strips):
            mine = mine + shifted(back[s], "tile", strips - s)
        return mine
    got = lax.all_to_all(
        back[0].reshape(strips, count, feat), "tile", split_axis=0, concat_axis=0, tiled=True
    )
    return jnp.sum(got.astype(jnp.float32), axis=0).astype(kernels.dtype)


def solution(mesh):
    return jax.shard_map(
        local,
        mesh=mesh,
        in_specs=(
            P(("groups", "tile"), None, None),
            P(("groups", "tile", "inst"), None),
            P(("groups", "tile", "inst"), None),
            P(("groups", "tile", "inst"), None),
            P(),
            P(None, "inst"),
            P("inst", None),
        ),
        out_specs=P(("groups", "tile", "inst"), None),
        check_vma=False,
    )
```

```python
import functools

import jax
import jax.numpy as jnp
from jax import lax
from jax.experimental import pallas as pl
from jax.experimental.pallas import tpu as pltpu
from jax.sharding import PartitionSpec as P

TS = 32
SR = 2
WC = 8
META = 16
ROWS_PER_STEP = 4
ARRIVALS = (16, 16, 32)
VMEM = pltpu.VMEM


def write_block(kernels_ref, home_ref, boxes_ref, out_ref):
    count = kernels_ref.shape[0]
    out_ref[:count, :] = kernels_ref[...]
    out_ref[count:, :] = jnp.zeros((META, out_ref.shape[1]), out_ref.dtype)
    line = lax.broadcasted_iota(jnp.int32, (META, count), 0)
    meta = jnp.where(line == 0, home_ref[...], 0)
    for i in range(4):
        meta = jnp.where(line == i + 1, boxes_ref[i : i + 1, :], meta)
    out_ref[count:, :count] = meta.astype(jnp.float32).astype(out_ref.dtype)


def pack_kernel(kernels_ref, home_ref, boxes_ref, w_in_hbm, w_out_hbm, block_ref, shard_ref, sems):
    hidden, feat = w_out_hbm.shape
    copies = [pltpu.make_async_copy(w_out_hbm, shard_ref.at[pl.ds(0, hidden)], sems.at[0])]
    for i in range(hidden // feat):
        copies.append(
            pltpu.make_async_copy(
                w_in_hbm.at[:, pl.ds(i * feat, feat)],
                shard_ref.at[pl.ds(hidden + i * feat, feat)],
                sems.at[i + 1],
            )
        )
    for copy in copies:
        copy.start()
    write_block(kernels_ref, home_ref, boxes_ref, block_ref)
    for copy in copies:
        copy.wait()


def pool_kernel(blocks, slots, count, *refs):
    block_refs, features_hbm, refs = refs[:blocks], refs[blocks], refs[blocks + 1 :]
    out_refs, (features_ref, sems) = refs[:-2], refs[-2:]
    bf16, f32 = jnp.bfloat16, jnp.float32
    mine = lax.axis_index("tile")
    stride, feat = count + META, block_refs[0].shape[1]
    steps = features_ref.shape[0] // ROWS_PER_STEP
    copies, at = {}, 0
    for i, size in enumerate(ARRIVALS):
        part = pl.ds(at, size)
        copies[at // ROWS_PER_STEP] = pltpu.make_async_copy(
            features_hbm.at[part], features_ref.at[part], sems.at[i]
        )
        copies[at // ROWS_PER_STEP].start()
        at += size

    sources = [(ref, i) for ref in block_refs for i in range(ref.shape[0] // stride)]
    earlier = (
        lax.broadcasted_iota(jnp.int32, (count, count), 0)
        < lax.broadcasted_iota(jnp.int32, (count, count), 1)
    ).astype(bf16)
    slot = lax.broadcasted_iota(jnp.int32, (slots, count), 0).astype(f32)
    base = jnp.zeros((1, 1), f32)
    rows = jnp.zeros((slots, feat), f32)
    bounds = jnp.zeros((slots, META), f32)
    select = [None] * len(sources)
    for k in range(len(sources)):
        ref, i = sources[k]
        meta = ref[i * stride + count : (i + 1) * stride, :count]
        member = jnp.where(meta[0:1].astype(f32) == mine.astype(f32), 1.0, 0.0)
        rank = jnp.dot(
            jnp.broadcast_to(member, (8, count)).astype(bf16), earlier, preferred_element_type=f32
        )[0:1]
        pick = jnp.where((rank + base == slot) & (member > 0.0), 1.0, 0.0)
        pick16 = pick.astype(bf16)
        rows = rows + jnp.dot(
            pick16, ref[i * stride : i * stride + count, :], preferred_element_type=f32
        )
        bounds = bounds + lax.dot_general(
            pick16, meta, (((1,), (1,)), ((), ())), preferred_element_type=f32
        )
        select[k] = pick.T.astype(bf16)
        base = base + jnp.sum(member, axis=1, keepdims=True)
    rows16 = rows.astype(bf16)

    width = WC * TS
    tile_col = (lax.broadcasted_iota(jnp.int32, (slots, width), 1) // TS).astype(f32)
    column = (bounds[:, 3:4] <= tile_col) & (tile_col <= bounds[:, 4:5])
    inside = [
        jnp.where(column & (bounds[:, 1:2] <= r) & (r <= bounds[:, 2:3]), 1.0, 0.0)
        for r in range(SR)
    ]

    def cells(step):
        return features_ref[step * ROWS_PER_STEP : (step + 1) * ROWS_PER_STEP].reshape(
            ROWS_PER_STEP * width, feat
        )

    def logits(step):
        if step in copies:
            copies[step].wait()
        return lax.dot_general(
            rows16, cells(step), (((1,), (1,)), ((), ())), preferred_element_type=f32
        )

    pooled = jnp.zeros((slots, feat), f32)
    covered = jnp.zeros((slots, width), f32)
    now = logits(0)
    for step in range(steps):
        later = logits(step + 1) if step + 1 < steps else None
        mask = inside[step * ROWS_PER_STEP // TS]
        parts = []
        for j in range(ROWS_PER_STEP):
            part = mask * pl.reciprocal(
                1.0 + jnp.exp(-now[:, j * width : (j + 1) * width]), approx=True
            )
            covered = covered + part
            parts.append(part.astype(bf16))
        pooled = pooled + jnp.dot(
            jnp.concatenate(parts, axis=1), cells(step), preferred_element_type=f32
        )
        now = later
    area = jnp.sum(covered, axis=1, keepdims=True)
    ratio = (pooled / area).astype(bf16)

    for k, pick in enumerate(select):
        back = jnp.dot(pick, ratio, preferred_element_type=f32).astype(bf16)
        ref, i = out_refs[k * len(out_refs) // len(select)], k % (len(select) // len(out_refs))
        ref[i * count : (i + 1) * count, :] = back


def through(normed, total, shard_refs):
    feat = total.shape[1]
    for ref in shard_refs:
        width = ref.shape[0] // 2
        for i in range(0, width, feat):
            hidden = jnp.dot(
                normed, ref[width + i : width + i + feat, :], preferred_element_type=jnp.float32
            )
            total = total + jnp.dot(
                jnp.maximum(hidden, 0.0).astype(normed.dtype),
                ref[i : i + feat, :],
                preferred_element_type=jnp.float32,
            )
    return total


def update_kernel(backs, shards, *refs):
    back_refs, refs = refs[:backs], refs[backs:]
    own_hbm, shard_refs, refs = refs[:2], refs[2 : 2 + shards], refs[2 + shards :]
    normed_ref, total_ref, kernels_ref, gain_ref, sems = refs
    own = (kernels_ref, gain_ref)
    f32 = jnp.float32
    copies = [pltpu.make_async_copy(a, b, sems.at[i]) for i, (a, b) in enumerate(zip(own_hbm, own))]
    for copy in copies:
        copy.start()
    ratio = back_refs[0][...].astype(f32)
    for ref in back_refs[1:]:
        ratio = ratio + ref[...].astype(f32)
    copies[0].wait()
    merged = kernels_ref[...].astype(f32) + ratio
    centred = merged - jnp.mean(merged, axis=1, keepdims=True)
    spread = jnp.mean(centred * centred, axis=1, keepdims=True)
    copies[1].wait()
    normed = (centred * lax.rsqrt(spread + 1e-05) * gain_ref[...]).astype(normed_ref.dtype)
    normed_ref[...] = normed
    total_ref[...] = through(normed, merged, shard_refs)


def finish_kernel(normed_ref, total_ref, *refs):
    out_ref = refs[-1]
    out_ref[...] = through(normed_ref[...], total_ref[...], refs[:-1]).astype(out_ref.dtype)


def exchanged(x, axis, distance):
    return lax.ppermute(x, axis, [(i, i ^ distance) for i in range(lax.axis_size(axis))])


def local(features, kernels, home, boxes, gain, w_in, w_out):
    strips, holders = lax.axis_size("tile"), lax.axis_size("inst")
    count, feat = kernels.shape
    slots = strips * min(count, max(2, 5 * count // (2 * strips)))
    near = strips <= 8
    any_, hbm = pl.BlockSpec(memory_space=VMEM), pl.BlockSpec(memory_space=pltpu.HBM)

    block, shard = pl.pallas_call(
        pack_kernel,
        out_shape=[
            pltpu.VMEM((count + META, feat), kernels.dtype),
            pltpu.VMEM((2 * w_out.shape[0], feat), w_out.dtype),
        ],
        in_specs=[any_] * 3 + [hbm] * 2,
        out_specs=[any_] * 2,
        scratch_shapes=[pltpu.SemaphoreType.DMA((1 + w_out.shape[0] // feat,))],
        name="pack",
    )(kernels, home.T, boxes.T, w_in, w_out)
    if near:
        blocks = [block] + [exchanged(block, "tile", d) for d in range(1, strips)]
        outs = [jax.ShapeDtypeStruct((count, feat), kernels.dtype)] * strips
    else:
        blocks = [lax.all_gather(block, "tile", axis=0, tiled=True)]
        outs = [jax.ShapeDtypeStruct((strips * count, feat), kernels.dtype)]

    shards = [shard]
    distance = holders // 2
    while distance > 1:
        shards += [exchanged(x, "inst", distance) for x in shards]
        distance //= 2

    back = pl.pallas_call(
        functools.partial(pool_kernel, len(blocks), slots, count),
        out_shape=outs,
        in_specs=[any_] * len(blocks) + [hbm],
        out_specs=[any_] * len(outs),
        scratch_shapes=[
            pltpu.VMEM(features.shape, features.dtype),
            pltpu.SemaphoreType.DMA((len(ARRIVALS),)),
        ],
        compiler_params=pltpu.CompilerParams(vmem_limit_bytes=48 << 20),
        cost_estimate=pl.CostEstimate(
            flops=40 * slots * features.size, bytes_accessed=2 * features.size, transcendentals=0
        ),
        name="pool",
    )(*blocks, features)
    if near:
        backs = [back[0]] + [exchanged(back[d], "tile", d) for d in range(1, strips)]
    else:
        got = lax.all_to_all(
            back[0].reshape(strips, count, feat), "tile", split_axis=0, concat_axis=0, tiled=True
        )
        backs = [jnp.sum(got.astype(jnp.float32), axis=0).astype(kernels.dtype)]

    late = [exchanged(x, "inst", 1) for x in shards]

    normed, total = pl.pallas_call(
        functools.partial(update_kernel, len(backs), len(shards)),
        out_shape=[
            jax.ShapeDtypeStruct((count, feat), kernels.dtype),
            jax.ShapeDtypeStruct((count, feat), jnp.float32),
        ],
        in_specs=[any_] * len(backs) + [hbm] * 2 + [any_] * len(shards),
        out_specs=[any_] * 2,
        scratch_shapes=[
            pltpu.VMEM((count, feat), kernels.dtype),
            pltpu.VMEM((1, feat), gain.dtype),
            pltpu.SemaphoreType.DMA((2,)),
        ],
        compiler_params=pltpu.CompilerParams(vmem_limit_bytes=48 << 20),
        cost_estimate=pl.CostEstimate(
            flops=40 * slots * features.size, bytes_accessed=2 * features.size, transcendentals=0
        ),
        name="update",
    )(*backs, kernels, gain.reshape(1, feat), *shards)
    return pl.pallas_call(
        finish_kernel,
        out_shape=jax.ShapeDtypeStruct((count, feat), kernels.dtype),
        in_specs=[any_] * (2 + len(late)),
        out_specs=any_,
        compiler_params=pltpu.CompilerParams(vmem_limit_bytes=48 << 20),
        name="finish",
    )(normed, total, *late)


def solution(mesh):
    return jax.shard_map(
        local,
        mesh=mesh,
        in_specs=(
            P(("groups", "tile"), None, None),
            P(("groups", "tile", "inst"), None),
            P(("groups", "tile", "inst"), None),
            P(("groups", "tile", "inst"), None),
            P(),
            P(None, "inst"),
            P("inst", None),
        ),
        out_specs=P(("groups", "tile", "inst"), None),
        check_vma=False,
    )
```

```python
import functools

import jax
import jax.numpy as jnp
from jax import lax
from jax.experimental import pallas as pl
from jax.experimental.pallas import tpu as pltpu
from jax.sharding import PartitionSpec as P

TS = 32
SR = 2
WC = 8
META = 8
ROWS_PER_STEP = 4
ARRIVALS = (16, 16, 32)
VMEM = pltpu.VMEM


def start_all(copies):
    for copy in copies:
        copy.start()
    return copies


def pack_kernel(near, groups, room, *refs):
    home_hbm, boxes_hbm, kernels_hbm, w_out_hbm, w_in_hbm, block_refs = *refs[:5], refs[5:-6]
    pick_ref, shard_ref, home_ref, boxes_ref, kernels_ref, sems = refs[-6:]
    bf16, f32 = jnp.bfloat16, jnp.float32
    count, feat = kernels_ref.shape
    hidden = w_out_hbm.shape[0]
    pairs = [(home_hbm, home_ref), (boxes_hbm, boxes_ref), (kernels_hbm, kernels_ref)]
    pairs.append((w_out_hbm, shard_ref.at[pl.ds(0, hidden)]))
    for i in range(hidden // feat):
        part = shard_ref.at[pl.ds(hidden + i * feat, feat)]
        pairs.append((w_in_hbm.at[:, pl.ds(i * feat, feat)], part))
    copies = start_all(
        [pltpu.make_async_copy(a, b, sems.at[i]) for i, (a, b) in enumerate(pairs)]
    )

    earlier = (
        lax.broadcasted_iota(jnp.int32, (count, count), 0)
        < lax.broadcasted_iota(jnp.int32, (count, count), 1)
    ).astype(bf16)
    rows = -(-groups // 8) * 8
    line = lax.broadcasted_iota(jnp.int32, (rows, count), 0)
    slot = lax.broadcasted_iota(jnp.int32, (groups * room, count), 0)
    copies[0].wait()
    group = home_ref[...]
    if near:
        group = group ^ lax.axis_index("tile")
    member = jnp.where(group == line, 1.0, 0.0)
    rank = jnp.dot(member.astype(bf16), earlier, preferred_element_type=f32)
    rank = jnp.sum(rank * member, axis=0, keepdims=True).astype(jnp.int32)
    select = jnp.where(group * room + rank == slot, 1.0, 0.0)
    select16 = select.astype(bf16)
    pick_ref[...] = select.T.astype(bf16)
    copies[1].wait()
    bounds = jnp.concatenate(
        [boxes_ref[...], jnp.zeros((META - boxes_ref.shape[0], count), jnp.int32)], axis=0
    )
    bounds = lax.dot_general(
        bounds.astype(f32).astype(bf16),
        select16,
        (((1,), (1,)), ((), ())),
        preferred_element_type=f32,
    )
    copies[2].wait()
    placed = jnp.dot(select16, kernels_ref[...], preferred_element_type=f32)
    stride = block_refs[0].shape[0] * len(block_refs) // groups
    for g in range(groups):
        ref, at = (block_refs[g], 0) if len(block_refs) > 1 else (block_refs[0], g * stride)
        part = slice(g * room, (g + 1) * room)
        ref[at : at + stride, :] = jnp.concatenate(
            [
                placed[part],
                jnp.concatenate([bounds[:, part], jnp.zeros((META, feat - room), f32)], axis=1),
            ]
            + [jnp.zeros((stride - room - META, feat), f32)] * (stride > room + META),
            axis=0,
        ).astype(bf16)
    for copy in copies[3:]:
        copy.wait()


def pool_kernel(blocks, groups, room, *refs):
    block_refs, features_hbm, refs = refs[:blocks], refs[blocks], refs[blocks + 1 :]
    out_refs, (features_ref, sems) = refs[:-2], refs[-2:]
    bf16, f32 = jnp.bfloat16, jnp.float32
    slots, feat = groups * room, features_ref.shape[2]
    steps = features_ref.shape[0] // ROWS_PER_STEP
    copies, at = {}, 0
    for i, size in enumerate(ARRIVALS):
        part = pl.ds(at, size)
        copies[at // ROWS_PER_STEP] = pltpu.make_async_copy(
            features_hbm.at[part], features_ref.at[part], sems.at[i]
        )
        copies[at // ROWS_PER_STEP].start()
        at += size

    stride = block_refs[0].shape[0] * blocks // groups
    unit = jnp.where(
        lax.broadcasted_iota(jnp.int32, (room, room), 0)
        == lax.broadcasted_iota(jnp.int32, (room, room), 1),
        1.0,
        0.0,
    ).astype(bf16)
    rows, bounds = [], []
    for g in range(groups):
        block = block_refs[g][...] if blocks > 1 else block_refs[0][g * stride : (g + 1) * stride, :]
        rows.append(block[:room].astype(f32))
        bounds.append(
            lax.dot_general(
                unit,
                block[room : room + META, :room],
                (((1,), (1,)), ((), ())),
                preferred_element_type=f32,
            )
        )
    rows16 = jnp.concatenate(rows, axis=0).astype(bf16)
    bounds = jnp.concatenate(bounds, axis=0)

    width = WC * TS
    tile_col = (lax.broadcasted_iota(jnp.int32, (slots, width), 1) // TS).astype(f32)
    column = (bounds[:, 2:3] <= tile_col) & (tile_col <= bounds[:, 3:4])
    inside = [
        jnp.where(column & (bounds[:, 0:1] <= r) & (r <= bounds[:, 1:2]), 1.0, 0.0)
        for r in range(SR)
    ]

    def cells(step):
        return features_ref[step * ROWS_PER_STEP : (step + 1) * ROWS_PER_STEP].reshape(
            ROWS_PER_STEP * width, feat
        )

    def logits(step):
        if step in copies:
            copies[step].wait()
        return lax.dot_general(
            rows16, cells(step), (((1,), (1,)), ((), ())), preferred_element_type=f32
        )

    pooled = jnp.zeros((slots, feat), f32)
    covered = jnp.zeros((slots, width), f32)
    now = logits(0)
    for step in range(steps):
        later = logits(step + 1) if step + 1 < steps else None
        mask = inside[step * ROWS_PER_STEP // TS]
        parts = []
        for j in range(ROWS_PER_STEP):
            part = mask * pl.reciprocal(
                1.0 + jnp.exp(-now[:, j * width : (j + 1) * width]), approx=True
            )
            covered = covered + part
            parts.append(part.astype(bf16))
        pooled = pooled + jnp.dot(
            jnp.concatenate(parts, axis=1), cells(step), preferred_element_type=f32
        )
        now = later
    area = jnp.sum(covered, axis=1, keepdims=True)
    ratio = (pooled / area).astype(bf16).astype(f32)

    for g in range(groups):
        part = ratio[g * room : (g + 1) * room]
        if len(out_refs) > 1:
            out_refs[g][...] = part.astype(bf16)
        else:
            out_refs[0][g * room : (g + 1) * room, :] = part.astype(bf16)


def through(normed, total, shard_refs):
    feat = total.shape[1]
    for ref in shard_refs:
        width = ref.shape[0] // 2
        for i in range(0, width, feat):
            hidden = jnp.dot(
                normed, ref[width + i : width + i + feat, :], preferred_element_type=jnp.float32
            )
            total = total + jnp.dot(
                jnp.maximum(hidden, 0.0).astype(normed.dtype),
                ref[i : i + feat, :],
                preferred_element_type=jnp.float32,
            )
    return total


def update_kernel(backs, shards, *refs):
    back_refs, pick_ref, refs = refs[:backs], refs[backs], refs[backs + 1 :]
    own_hbm, shard_refs, refs = refs[:2], refs[2 : 2 + shards], refs[2 + shards :]
    normed_ref, total_ref, kernels_ref, gain_ref, sems = refs
    own = (kernels_ref, gain_ref)
    f32 = jnp.float32
    copies = start_all(
        [pltpu.make_async_copy(a, b, sems.at[i]) for i, (a, b) in enumerate(zip(own_hbm, own))]
    )
    back = jnp.concatenate([ref[...].astype(f32) for ref in back_refs], axis=0)
    ratio = jnp.dot(pick_ref[...], back.astype(pick_ref.dtype), preferred_element_type=f32)
    copies[0].wait()
    merged = kernels_ref[...].astype(f32) + ratio
    centred = merged - jnp.mean(merged, axis=1, keepdims=True)
    spread = jnp.mean(centred * centred, axis=1, keepdims=True)
    copies[1].wait()
    normed = (centred * lax.rsqrt(spread + 1e-05) * gain_ref[...]).astype(normed_ref.dtype)
    normed_ref[...] = normed
    total_ref[...] = through(normed, merged, shard_refs)


def finish_kernel(normed_ref, total_ref, *refs):
    out_ref = refs[-1]
    out_ref[...] = through(normed_ref[...], total_ref[...], refs[:-1]).astype(out_ref.dtype)


def exchanged(x, axis, distance):
    return lax.ppermute(x, axis, [(i, i ^ distance) for i in range(lax.axis_size(axis))])


def local(features, kernels, home, boxes, gain, w_in, w_out):
    strips, holders = lax.axis_size("tile"), lax.axis_size("inst")
    count, feat = kernels.shape
    hidden = w_out.shape[0]
    most = min(count, max(2, 5 * count // (2 * strips)))
    room = -(-most // 8) * 8
    stride = -(-(room + META) // 16) * 16
    slots = strips * room
    near = strips & (strips - 1) == 0 and strips <= 8
    any_, hbm = pl.BlockSpec(memory_space=VMEM), pl.BlockSpec(memory_space=pltpu.HBM)

    parts = strips if near else 1
    *blocks, pick, shard = pl.pallas_call(
        functools.partial(pack_kernel, near, strips, room),
        out_shape=[pltpu.VMEM((strips // parts * stride, feat), kernels.dtype)] * parts
        + [
            pltpu.VMEM((count, slots), kernels.dtype),
            pltpu.VMEM((2 * hidden, feat), w_out.dtype),
        ],
        in_specs=[hbm] * 5,
        out_specs=[any_] * (parts + 2),
        scratch_shapes=[
            pltpu.VMEM((1, count), home.dtype),
            pltpu.VMEM((boxes.shape[1], count), boxes.dtype),
            pltpu.VMEM((count, feat), kernels.dtype),
            pltpu.SemaphoreType.DMA((4 + hidden // feat,)),
        ],
        name="pack",
    )(home.T, boxes.T, kernels, w_out, w_in)
    if near:
        blocks = [blocks[0]] + [exchanged(blocks[d], "tile", d) for d in range(1, strips)]
        outs = [jax.ShapeDtypeStruct((room, feat), kernels.dtype)] * strips
    else:
        got = lax.all_to_all(
            blocks[0].reshape(strips, stride, feat), "tile", split_axis=0, concat_axis=0, tiled=True
        )
        blocks = [got.reshape(strips * stride, feat)]
        outs = [jax.ShapeDtypeStruct((slots, feat), kernels.dtype)]

    shards = [shard]
    distance = holders // 2
    while distance > 1:
        shards += [exchanged(x, "inst", distance) for x in shards]
        distance //= 2

    back = pl.pallas_call(
        functools.partial(pool_kernel, len(blocks), strips, room),
        out_shape=outs,
        in_specs=[any_] * len(blocks) + [hbm],
        out_specs=[any_] * len(outs),
        scratch_shapes=[
            pltpu.VMEM(features.shape, features.dtype),
            pltpu.SemaphoreType.DMA((len(ARRIVALS),)),
        ],
        compiler_params=pltpu.CompilerParams(vmem_limit_bytes=48 << 20),
        cost_estimate=pl.CostEstimate(
            flops=40 * slots * features.size, bytes_accessed=2 * features.size, transcendentals=0
        ),
        name="pool",
    )(*blocks, features)
    if near:
        backs = [back[0]] + [exchanged(back[d], "tile", d) for d in range(1, strips)]
    else:
        got = lax.all_to_all(
            back[0].reshape(strips, room, feat), "tile", split_axis=0, concat_axis=0, tiled=True
        )
        backs = [got.reshape(slots, feat)]
    late = [exchanged(x, "inst", 1) for x in shards]

    normed, total = pl.pallas_call(
        functools.partial(update_kernel, len(backs), len(shards)),
        out_shape=[
            jax.ShapeDtypeStruct((count, feat), kernels.dtype),
            jax.ShapeDtypeStruct((count, feat), jnp.float32),
        ],
        in_specs=[any_] * (len(backs) + 1) + [hbm] * 2 + [any_] * len(shards),
        out_specs=[any_] * 2,
        scratch_shapes=[
            pltpu.VMEM((count, feat), kernels.dtype),
            pltpu.VMEM((1, feat), gain.dtype),
            pltpu.SemaphoreType.DMA((2,)),
        ],
        compiler_params=pltpu.CompilerParams(vmem_limit_bytes=48 << 20),
        cost_estimate=pl.CostEstimate(
            flops=40 * slots * features.size, bytes_accessed=2 * features.size, transcendentals=0
        ),
        name="update",
    )(*backs, pick, kernels, gain.reshape(1, feat), *shards)
    return pl.pallas_call(
        finish_kernel,
        out_shape=jax.ShapeDtypeStruct((count, feat), kernels.dtype),
        in_specs=[any_] * (2 + len(late)),
        out_specs=any_,
        compiler_params=pltpu.CompilerParams(vmem_limit_bytes=48 << 20),
        name="finish",
    )(normed, total, *late)


def solution(mesh):
    return jax.shard_map(
        local,
        mesh=mesh,
        in_specs=(
            P(("groups", "tile"), None, None),
            P(("groups", "tile", "inst"), None),
            P(("groups", "tile", "inst"), None),
            P(("groups", "tile", "inst"), None),
            P(),
            P(None, "inst"),
            P("inst", None),
        ),
        out_specs=P(("groups", "tile", "inst"), None),
        check_vma=False,
    )
```

```python
import functools

import jax
import jax.numpy as jnp
from jax import lax
from jax.experimental import pallas as pl
from jax.experimental.pallas import tpu as pltpu
from jax.sharding import PartitionSpec as P

TS = 32
SR = 2
WC = 8
META = 8
ROWS_PER_STEP = 4
VMEM = pltpu.VMEM


def start_all(copies):
    for copy in copies:
        copy.start()
    return copies


def pack_kernel(near, groups, room, *refs):
    home_hbm, boxes_hbm, kernels_hbm, w_out_hbm, w_in_hbm, block_refs = *refs[:5], refs[5:-6]
    pick_ref, shard_ref, home_ref, boxes_ref, kernels_ref, sems = refs[-6:]
    bf16, f32 = jnp.bfloat16, jnp.float32
    count, feat = kernels_ref.shape
    hidden = w_out_hbm.shape[0]
    pairs = [(home_hbm, home_ref), (boxes_hbm, boxes_ref), (kernels_hbm, kernels_ref)]
    pairs.append((w_out_hbm, shard_ref.at[pl.ds(0, hidden)]))
    for i in range(hidden // feat):
        part = shard_ref.at[pl.ds(hidden + i * feat, feat)]
        pairs.append((w_in_hbm.at[:, pl.ds(i * feat, feat)], part))
    copies = start_all(
        [pltpu.make_async_copy(a, b, sems.at[i]) for i, (a, b) in enumerate(pairs)]
    )

    earlier = (
        lax.broadcasted_iota(jnp.int32, (count, count), 0)
        < lax.broadcasted_iota(jnp.int32, (count, count), 1)
    ).astype(bf16)
    rows = -(-groups // 8) * 8
    line = lax.broadcasted_iota(jnp.int32, (rows, count), 0)
    slot = lax.broadcasted_iota(jnp.int32, (groups * room, count), 0)
    copies[0].wait()
    group = home_ref[...]
    if near:
        group = group ^ lax.axis_index("tile")
    member = jnp.where(group == line, 1.0, 0.0)
    rank = jnp.dot(member.astype(bf16), earlier, preferred_element_type=f32)
    rank = jnp.sum(rank * member, axis=0, keepdims=True).astype(jnp.int32)
    select = jnp.where(group * room + rank == slot, 1.0, 0.0)
    select16 = select.astype(bf16)
    pick_ref[...] = select.T.astype(bf16)
    copies[1].wait()
    bounds = jnp.concatenate(
        [boxes_ref[...], jnp.zeros((META - boxes_ref.shape[0], count), jnp.int32)], axis=0
    )
    bounds = lax.dot_general(
        bounds.astype(f32).astype(bf16),
        select16,
        (((1,), (1,)), ((), ())),
        preferred_element_type=f32,
    )
    copies[2].wait()
    placed = jnp.dot(select16, kernels_ref[...], preferred_element_type=f32)
    stride = block_refs[0].shape[0] * len(block_refs) // groups
    for g in range(groups):
        ref, at = (block_refs[g], 0) if len(block_refs) > 1 else (block_refs[0], g * stride)
        part = slice(g * room, (g + 1) * room)
        ref[at : at + stride, :] = jnp.concatenate(
            [
                placed[part],
                jnp.concatenate([bounds[:, part], jnp.zeros((META, feat - room), f32)], axis=1),
            ]
            + [jnp.zeros((stride - room - META, feat), f32)] * (stride > room + META),
            axis=0,
        ).astype(bf16)
    for copy in copies[3:]:
        copy.wait()


def pool_kernel(blocks, groups, room, *refs):
    block_refs, features_ref, out_refs = refs[:blocks][::-1], refs[blocks], refs[blocks + 1 :]
    bf16, f32 = jnp.bfloat16, jnp.float32
    slots, feat = groups * room, features_ref.shape[2]
    steps = features_ref.shape[0] // ROWS_PER_STEP
    stride = block_refs[0].shape[0] * blocks // groups
    unit = jnp.where(
        lax.broadcasted_iota(jnp.int32, (room, room), 0)
        == lax.broadcasted_iota(jnp.int32, (room, room), 1),
        1.0,
        0.0,
    ).astype(bf16)
    rows, bounds = [], []
    for g in range(groups):
        block = block_refs[g][...] if blocks > 1 else block_refs[0][g * stride : (g + 1) * stride, :]
        rows.append(block[:room].astype(f32))
        bounds.append(
            lax.dot_general(
                unit,
                block[room : room + META, :room],
                (((1,), (1,)), ((), ())),
                preferred_element_type=f32,
            )
        )
    rows16 = jnp.concatenate(rows, axis=0).astype(bf16)
    bounds = jnp.concatenate(bounds, axis=0)

    width = WC * TS
    tile_col = (lax.broadcasted_iota(jnp.int32, (slots, width), 1) // TS).astype(f32)
    column = (bounds[:, 2:3] <= tile_col) & (tile_col <= bounds[:, 3:4])
    inside = [
        jnp.where(column & (bounds[:, 0:1] <= r) & (r <= bounds[:, 1:2]), 1.0, 0.0)
        for r in range(SR)
    ]

    def cells(step):
        return features_ref[step * ROWS_PER_STEP : (step + 1) * ROWS_PER_STEP].reshape(
            ROWS_PER_STEP * width, feat
        )

    def logits(step):
        return lax.dot_general(
            rows16, cells(step), (((1,), (1,)), ((), ())), preferred_element_type=f32
        )

    pooled = jnp.zeros((slots, feat), f32)
    covered = jnp.zeros((slots, width), f32)
    now = logits(0)
    for step in range(steps):
        later = logits(step + 1) if step + 1 < steps else None
        mask = inside[step * ROWS_PER_STEP // TS]
        parts = []
        for j in range(ROWS_PER_STEP):
            part = mask * pl.reciprocal(
                1.0 + jnp.exp(-now[:, j * width : (j + 1) * width]), approx=True
            )
            covered = covered + part
            parts.append(part.astype(bf16))
        pooled = pooled + jnp.dot(
            jnp.concatenate(parts, axis=1), cells(step), preferred_element_type=f32
        )
        now = later
    area = jnp.sum(covered, axis=1, keepdims=True)
    ratio = (pooled / area).astype(bf16).astype(f32)

    for g in range(groups):
        part = ratio[g * room : (g + 1) * room]
        if len(out_refs) > 1:
            out_refs[g][...] = part.astype(bf16)
        else:
            out_refs[0][g * room : (g + 1) * room, :] = part.astype(bf16)


def through(normed, total, shard_refs):
    feat = total.shape[1]
    for ref in shard_refs:
        width = ref.shape[0] // 2
        for i in range(0, width, feat):
            hidden = jnp.dot(
                normed, ref[width + i : width + i + feat, :], preferred_element_type=jnp.float32
            )
            total = total + jnp.dot(
                jnp.maximum(hidden, 0.0).astype(normed.dtype),
                ref[i : i + feat, :],
                preferred_element_type=jnp.float32,
            )
    return total


def update_kernel(backs, shards, *refs):
    back_refs, pick_ref, refs = refs[:backs], refs[backs], refs[backs + 1 :]
    (kernels_ref, gain_ref), shard_refs, refs = refs[:2], refs[2 : 2 + shards], refs[2 + shards :]
    normed_ref, total_ref = refs
    f32 = jnp.float32
    back = jnp.concatenate([ref[...].astype(f32) for ref in back_refs[::-1]], axis=0)
    ratio = jnp.dot(pick_ref[...], back.astype(pick_ref.dtype), preferred_element_type=f32)
    merged = kernels_ref[...].astype(f32) + ratio
    centred = merged - jnp.mean(merged, axis=1, keepdims=True)
    spread = jnp.mean(centred * centred, axis=1, keepdims=True)
    normed = (centred * lax.rsqrt(spread + 1e-05) * gain_ref[...]).astype(normed_ref.dtype)
    normed_ref[...] = normed
    total_ref[...] = through(normed, merged, shard_refs)


def finish_kernel(normed_ref, total_ref, *refs):
    out_ref = refs[-1]
    out_ref[...] = through(normed_ref[...], total_ref[...], refs[:-1]).astype(out_ref.dtype)


def exchanged(x, axis, distance):
    return lax.ppermute(x, axis, [(i, i ^ distance) for i in range(lax.axis_size(axis))])


def all_exchanged(xs):
    strips, holders = lax.axis_size("tile"), lax.axis_size("inst")
    beside = 1 if holders % 2 == 0 else 0
    pairs = [(t, i) for t in range(strips) for i in range(holders)]
    return [
        lax.ppermute(
            xs[d],
            ("tile", "inst"),
            [(t * holders + i, (t ^ d) * holders + (i ^ beside)) for t, i in pairs],
        )
        for d in range(len(xs) - 1, 0, -1)
    ]


def local(features, kernels, home, boxes, gain, w_in, w_out):
    strips, holders = lax.axis_size("tile"), lax.axis_size("inst")
    count, feat = kernels.shape
    hidden = w_out.shape[0]
    most = min(count, max(2, 5 * count // (2 * strips)))
    room = -(-most // 8) * 8
    stride = -(-(room + META) // 16) * 16
    slots = strips * room
    near = strips & (strips - 1) == 0 and strips <= 8
    any_, hbm = pl.BlockSpec(memory_space=VMEM), pl.BlockSpec(memory_space=pltpu.HBM)

    parts = strips if near else 1
    *blocks, pick, shard = pl.pallas_call(
        functools.partial(pack_kernel, near, strips, room),
        out_shape=[pltpu.VMEM((strips // parts * stride, feat), kernels.dtype)] * parts
        + [
            pltpu.VMEM((count, slots), kernels.dtype),
            pltpu.VMEM((2 * hidden, feat), w_out.dtype),
        ],
        in_specs=[hbm] * 5,
        out_specs=[any_] * (parts + 2),
        scratch_shapes=[
            pltpu.VMEM((1, count), home.dtype),
            pltpu.VMEM((boxes.shape[1], count), boxes.dtype),
            pltpu.VMEM((count, feat), kernels.dtype),
            pltpu.SemaphoreType.DMA((4 + hidden // feat,)),
        ],
        cost_estimate=pl.CostEstimate(
            flops=40 * slots * features.size, bytes_accessed=2 * features.size, transcendentals=0
        ),
        compiler_params=pltpu.CompilerParams(vmem_limit_bytes=24 << 20),
        name="pack",
    )(*[pltpu.with_memory_space_constraint(x, pltpu.HBM) for x in (home.T, boxes.T, kernels, w_out, w_in)])
    if near:
        blocks = all_exchanged(blocks) + [blocks[0]]
        outs = [jax.ShapeDtypeStruct((room, feat), kernels.dtype)] * strips
    else:
        got = lax.all_to_all(
            blocks[0].reshape(strips, stride, feat), "tile", split_axis=0, concat_axis=0, tiled=True
        )
        blocks = [got.reshape(strips * stride, feat)]
        outs = [jax.ShapeDtypeStruct((slots, feat), kernels.dtype)]

    shards = [shard]
    distance = holders // 2
    while distance > 1:
        shards += [exchanged(x, "inst", distance) for x in shards]
        distance //= 2

    back = pl.pallas_call(
        functools.partial(pool_kernel, len(blocks), strips, room),
        out_shape=outs,
        in_specs=[any_] * (len(blocks) + 1),
        out_specs=[any_] * len(outs),
        compiler_params=pltpu.CompilerParams(vmem_limit_bytes=24 << 20),
        cost_estimate=pl.CostEstimate(
            flops=40 * slots * features.size, bytes_accessed=2 * features.size, transcendentals=0
        ),
        name="pool",
    )(*blocks, features)
    if near:
        backs = all_exchanged(back) + [back[0]]
    else:
        got = lax.all_to_all(
            back[0].reshape(strips, room, feat), "tile", split_axis=0, concat_axis=0, tiled=True
        )
        backs = [got.reshape(slots, feat)]
    late = [exchanged(x, "inst", 1) for x in shards]

    normed, total = pl.pallas_call(
        functools.partial(update_kernel, len(backs), len(shards)),
        out_shape=[
            jax.ShapeDtypeStruct((count, feat), kernels.dtype),
            jax.ShapeDtypeStruct((count, feat), jnp.float32),
        ],
        in_specs=[any_] * (len(backs) + 3 + len(shards)),
        out_specs=[any_] * 2,
        compiler_params=pltpu.CompilerParams(vmem_limit_bytes=24 << 20),
        cost_estimate=pl.CostEstimate(
            flops=40 * slots * features.size, bytes_accessed=2 * features.size, transcendentals=0
        ),
        name="update",
    )(*backs, pick, kernels, gain.reshape(1, feat), *shards)
    return pl.pallas_call(
        finish_kernel,
        out_shape=jax.ShapeDtypeStruct((count, feat), kernels.dtype),
        in_specs=[any_] * (2 + len(late)),
        out_specs=any_,
        compiler_params=pltpu.CompilerParams(vmem_limit_bytes=24 << 20),
        name="finish",
    )(normed, total, *late)


def solution(mesh):
    return jax.shard_map(
        local,
        mesh=mesh,
        in_specs=(
            P(("groups", "tile"), None, None),
            P(("groups", "tile", "inst"), None),
            P(("groups", "tile", "inst"), None),
            P(("groups", "tile", "inst"), None),
            P(),
            P(None, "inst"),
            P("inst", None),
        ),
        out_specs=P(("groups", "tile", "inst"), None),
        check_vma=False,
    )
```

```python
import functools

import jax
import jax.numpy as jnp
from jax import lax
from jax.experimental import pallas as pl
from jax.experimental.pallas import tpu as pltpu
from jax.sharding import PartitionSpec as P

TS = 32
SR = 2
WC = 8
META = 8
ROWS_PER_STEP = 4
VMEM = pltpu.VMEM


def start_all(copies):
    for copy in copies:
        copy.start()
    return copies


def pack_kernel(near, groups, room, *refs):
    home_hbm, boxes_hbm, kernels_hbm, w_out_hbm, w_in_hbm, block_refs = *refs[:5], refs[5:-6]
    at_ref, shard_ref, home_ref, boxes_ref, kernels_ref, sems = refs[-6:]
    bf16, f32 = jnp.bfloat16, jnp.float32
    count, feat = kernels_ref.shape
    hidden = w_out_hbm.shape[0]
    pairs = [(home_hbm, home_ref), (boxes_hbm, boxes_ref), (kernels_hbm, kernels_ref)]
    pairs.append((w_out_hbm, shard_ref.at[pl.ds(0, hidden)]))
    for i in range(hidden // feat):
        part = shard_ref.at[pl.ds(hidden + i * feat, feat)]
        pairs.append((w_in_hbm.at[:, pl.ds(i * feat, feat)], part))
    copies = start_all(
        [pltpu.make_async_copy(a, b, sems.at[i]) for i, (a, b) in enumerate(pairs)]
    )

    earlier = (
        lax.broadcasted_iota(jnp.int32, (count, count), 0)
        < lax.broadcasted_iota(jnp.int32, (count, count), 1)
    ).astype(bf16)
    rows = -(-groups // 8) * 8
    line = lax.broadcasted_iota(jnp.int32, (rows, count), 0)
    slot = lax.broadcasted_iota(jnp.int32, (groups * room, count), 0)
    copies[0].wait()
    group = home_ref[...]
    if near:
        group = group ^ lax.axis_index("tile")
    member = jnp.where(group == line, 1.0, 0.0)
    rank = jnp.dot(member.astype(bf16), earlier, preferred_element_type=f32)
    rank = jnp.sum(rank * member, axis=0, keepdims=True).astype(jnp.int32)
    at = group * room + rank
    select16 = jnp.where(at == slot, 1.0, 0.0).astype(bf16)
    at_ref[...] = jnp.broadcast_to(at, at_ref.shape)
    copies[1].wait()
    bounds = jnp.concatenate(
        [boxes_ref[...], jnp.zeros((META - boxes_ref.shape[0], count), jnp.int32)], axis=0
    )
    bounds = lax.dot_general(
        bounds.astype(f32).astype(bf16),
        select16,
        (((1,), (1,)), ((), ())),
        preferred_element_type=f32,
    )
    copies[2].wait()
    placed = jnp.dot(select16, kernels_ref[...], preferred_element_type=f32)
    stride = block_refs[0].shape[0] * len(block_refs) // groups
    for g in range(groups):
        ref, at = (block_refs[g], 0) if len(block_refs) > 1 else (block_refs[0], g * stride)
        part = slice(g * room, (g + 1) * room)
        ref[at : at + stride, :] = jnp.concatenate(
            [
                placed[part],
                jnp.concatenate([bounds[:, part], jnp.zeros((META, feat - room), f32)], axis=1),
            ]
            + [jnp.zeros((stride - room - META, feat), f32)] * (stride > room + META),
            axis=0,
        ).astype(bf16)
    for copy in copies[3:]:
        copy.wait()


def pool_kernel(blocks, groups, room, *refs):
    block_refs, features_ref, out_refs = refs[:blocks][::-1], refs[blocks], refs[blocks + 1 :]
    bf16, f32 = jnp.bfloat16, jnp.float32
    slots, feat = groups * room, features_ref.shape[2]
    steps = features_ref.shape[0] // ROWS_PER_STEP
    stride = block_refs[0].shape[0] * blocks // groups
    unit = jnp.where(
        lax.broadcasted_iota(jnp.int32, (room, room), 0)
        == lax.broadcasted_iota(jnp.int32, (room, room), 1),
        1.0,
        0.0,
    ).astype(bf16)
    rows, bounds = [], []
    for g in range(groups):
        block = block_refs[g][...] if blocks > 1 else block_refs[0][g * stride : (g + 1) * stride, :]
        rows.append(block[:room].astype(f32))
        bounds.append(
            lax.dot_general(
                unit,
                block[room : room + META, :room],
                (((1,), (1,)), ((), ())),
                preferred_element_type=f32,
            )
        )
    rows16 = jnp.concatenate(rows, axis=0).astype(bf16)
    bounds = jnp.concatenate(bounds, axis=0)

    width = WC * TS
    tile_col = (lax.broadcasted_iota(jnp.int32, (slots, width), 1) // TS).astype(f32)
    column = (bounds[:, 2:3] <= tile_col) & (tile_col <= bounds[:, 3:4])
    inside = [
        jnp.where(column & (bounds[:, 0:1] <= r) & (r <= bounds[:, 1:2]), 1.0, 0.0)
        for r in range(SR)
    ]

    def cells(step):
        return features_ref[step * ROWS_PER_STEP : (step + 1) * ROWS_PER_STEP].reshape(
            ROWS_PER_STEP * width, feat
        )

    def logits(step):
        return lax.dot_general(
            rows16, cells(step), (((1,), (1,)), ((), ())), preferred_element_type=f32
        )

    pooled = jnp.zeros((slots, feat), f32)
    covered = jnp.zeros((slots, width), f32)
    now = logits(0)
    for step in range(steps):
        later = logits(step + 1) if step + 1 < steps else None
        mask = inside[step * ROWS_PER_STEP // TS]
        parts = []
        for j in range(ROWS_PER_STEP):
            part = mask * pl.reciprocal(
                1.0 + jnp.exp(-now[:, j * width : (j + 1) * width]), approx=True
            )
            covered = covered + part
            parts.append(part.astype(bf16))
        pooled = pooled + jnp.dot(
            jnp.concatenate(parts, axis=1), cells(step), preferred_element_type=f32
        )
        now = later
    area = jnp.sum(covered, axis=1, keepdims=True)
    ratio = (pooled / area).astype(bf16).astype(f32)

    if len(out_refs) > 1:
        for g in range(groups):
            out_refs[g][...] = ratio[g * room : (g + 1) * room].astype(bf16)
    else:
        out_refs[0][...] = ratio.astype(bf16)


def place_kernel(at_ref, pick_ref):
    count, slots = pick_ref.shape
    slot = lax.broadcasted_iota(jnp.int32, (slots, count), 0)
    pick_ref[...] = jnp.where(at_ref[:1, :] == slot, 1.0, 0.0).T.astype(pick_ref.dtype)


def through(normed, total, shard_refs):
    feat = total.shape[1]
    for ref in shard_refs:
        width = ref.shape[0] // 2
        for i in range(0, width, feat):
            hidden = jnp.dot(
                normed, ref[width + i : width + i + feat, :], preferred_element_type=jnp.float32
            )
            total = total + jnp.dot(
                jnp.maximum(hidden, 0.0).astype(normed.dtype),
                ref[i : i + feat, :],
                preferred_element_type=jnp.float32,
            )
    return total


def update_kernel(backs, shards, *refs):
    back_refs, pick_ref, refs = refs[:backs], refs[backs], refs[backs + 1 :]
    (kernels_ref, gain_ref), shard_refs, refs = refs[:2], refs[2 : 2 + shards], refs[2 + shards :]
    normed_ref, total_ref = refs
    f32 = jnp.float32
    back = jnp.concatenate([ref[...].astype(f32) for ref in back_refs[::-1]], axis=0)
    ratio = jnp.dot(pick_ref[...], back.astype(pick_ref.dtype), preferred_element_type=f32)
    merged = kernels_ref[...].astype(f32) + ratio
    centred = merged - jnp.mean(merged, axis=1, keepdims=True)
    spread = jnp.mean(centred * centred, axis=1, keepdims=True)
    normed = (centred * lax.rsqrt(spread + 1e-05) * gain_ref[...]).astype(normed_ref.dtype)
    normed_ref[...] = normed
    total_ref[...] = through(normed, merged, shard_refs)


def finish_kernel(normed_ref, total_ref, *refs):
    out_ref = refs[-1]
    out_ref[...] = through(normed_ref[...], total_ref[...], refs[:-1]).astype(out_ref.dtype)


def exchanged(x, axis, distance):
    return lax.ppermute(x, axis, [(i, i ^ distance) for i in range(lax.axis_size(axis))])


def all_exchanged(xs):
    strips, holders = lax.axis_size("tile"), lax.axis_size("inst")
    beside = 1 if holders % 2 == 0 else 0
    pairs = [(t, i) for t in range(strips) for i in range(holders)]
    return [
        lax.ppermute(
            xs[d],
            ("tile", "inst"),
            [(t * holders + i, (t ^ d) * holders + (i ^ beside)) for t, i in pairs],
        )
        for d in range(len(xs) - 1, 0, -1)
    ]


def local(features, kernels, home, boxes, gain, w_in, w_out):
    strips, holders = lax.axis_size("tile"), lax.axis_size("inst")
    count, feat = kernels.shape
    hidden = w_out.shape[0]
    most = min(count, max(2, 5 * count // (2 * strips)))
    room = -(-most // 8) * 8
    stride = -(-(room + META) // 16) * 16
    slots = strips * room
    near = strips & (strips - 1) == 0 and strips <= 8
    any_, hbm = pl.BlockSpec(memory_space=VMEM), pl.BlockSpec(memory_space=pltpu.HBM)

    parts = strips if near else 1
    *blocks, places, shard = pl.pallas_call(
        functools.partial(pack_kernel, near, strips, room),
        out_shape=[pltpu.VMEM((strips // parts * stride, feat), kernels.dtype)] * parts
        + [
            pltpu.VMEM((count, count), jnp.int32),
            pltpu.VMEM((2 * hidden, feat), w_out.dtype),
        ],
        in_specs=[hbm] * 5,
        out_specs=[any_] * (parts + 2),
        scratch_shapes=[
            pltpu.VMEM((1, count), home.dtype),
            pltpu.VMEM((boxes.shape[1], count), boxes.dtype),
            pltpu.VMEM((count, feat), kernels.dtype),
            pltpu.SemaphoreType.DMA((4 + hidden // feat,)),
        ],
        cost_estimate=pl.CostEstimate(
            flops=40 * slots * features.size, bytes_accessed=2 * features.size, transcendentals=0
        ),
        compiler_params=pltpu.CompilerParams(vmem_limit_bytes=24 << 20),
        name="pack",
    )(*[pltpu.with_memory_space_constraint(x, pltpu.HBM) for x in (home.T, boxes.T, kernels, w_out, w_in)])
    if near:
        blocks = all_exchanged(blocks) + [blocks[0]]
        outs = [jax.ShapeDtypeStruct((room, feat), kernels.dtype)] * strips
    else:
        got = lax.all_to_all(
            blocks[0].reshape(strips, stride, feat), "tile", split_axis=0, concat_axis=0, tiled=True
        )
        blocks = [got.reshape(strips * stride, feat)]
        outs = [jax.ShapeDtypeStruct((slots, feat), kernels.dtype)]

    shards = [shard]
    distance = holders // 2
    while distance > 1:
        shards += [exchanged(x, "inst", distance) for x in shards]
        distance //= 2

    back = pl.pallas_call(
        functools.partial(pool_kernel, len(blocks), strips, room),
        out_shape=outs,
        in_specs=[any_] * (len(blocks) + 1),
        out_specs=[any_] * len(outs),
        compiler_params=pltpu.CompilerParams(vmem_limit_bytes=24 << 20),
        cost_estimate=pl.CostEstimate(
            flops=40 * slots * features.size, bytes_accessed=2 * features.size, transcendentals=0
        ),
        name="pool",
    )(*blocks, features)
    if near:
        backs = all_exchanged(back) + [back[0]]
    else:
        got = lax.all_to_all(
            back[0].reshape(strips, room, feat), "tile", split_axis=0, concat_axis=0, tiled=True
        )
        backs = [got.reshape(slots, feat)]
    pick = pl.pallas_call(
        place_kernel,
        out_shape=pltpu.VMEM((count, slots), kernels.dtype),
        in_specs=[any_],
        out_specs=any_,
        compiler_params=pltpu.CompilerParams(vmem_limit_bytes=24 << 20),
        name="place",
    )(places)
    late = [exchanged(x, "inst", 1) for x in shards]
    shards.insert(1, late.pop(0))

    normed, total = pl.pallas_call(
        functools.partial(update_kernel, len(backs), len(shards)),
        out_shape=[
            jax.ShapeDtypeStruct((count, feat), kernels.dtype),
            jax.ShapeDtypeStruct((count, feat), jnp.float32),
        ],
        in_specs=[any_] * (len(backs) + 3 + len(shards)),
        out_specs=[any_] * 2,
        compiler_params=pltpu.CompilerParams(vmem_limit_bytes=24 << 20),
        cost_estimate=pl.CostEstimate(
            flops=40 * slots * features.size, bytes_accessed=2 * features.size, transcendentals=0
        ),
        name="update",
    )(*backs, pick, kernels, gain.reshape(1, feat), *shards)
    return pl.pallas_call(
        finish_kernel,
        out_shape=jax.ShapeDtypeStruct((count, feat), kernels.dtype),
        in_specs=[any_] * (2 + len(late)),
        out_specs=any_,
        compiler_params=pltpu.CompilerParams(vmem_limit_bytes=24 << 20),
        name="finish",
    )(normed, total, *late)


def solution(mesh):
    return jax.shard_map(
        local,
        mesh=mesh,
        in_specs=(
            P(("groups", "tile"), None, None),
            P(("groups", "tile", "inst"), None),
            P(("groups", "tile", "inst"), None),
            P(("groups", "tile", "inst"), None),
            P(),
            P(None, "inst"),
            P("inst", None),
        ),
        out_specs=P(("groups", "tile", "inst"), None),
        check_vma=False,
    )
```

```python
import functools

import jax
import jax.numpy as jnp
from jax import lax
from jax.experimental import pallas as pl
from jax.experimental.pallas import tpu as pltpu
from jax.sharding import PartitionSpec as P

TS = 32
SR = 2
WC = 8
META = 8
ROWS_PER_STEP = 4
VMEM = pltpu.VMEM


def start_all(copies):
    for copy in copies:
        copy.start()
    return copies


def pack_kernel(near, groups, room, *refs):
    home_hbm, boxes_hbm, kernels_hbm, w_out_hbm, w_in_hbm, block_refs = *refs[:5], refs[5:-6]
    at_ref, shard_ref, home_ref, boxes_ref, kernels_ref, sems = refs[-6:]
    bf16, f32 = jnp.bfloat16, jnp.float32
    count, feat = kernels_ref.shape
    hidden = w_out_hbm.shape[0]
    pairs = [(home_hbm, home_ref), (boxes_hbm, boxes_ref), (kernels_hbm, kernels_ref)]
    pairs.append((w_out_hbm, shard_ref.at[pl.ds(0, hidden)]))
    for i in range(hidden // feat):
        part = shard_ref.at[pl.ds(hidden + i * feat, feat)]
        pairs.append((w_in_hbm.at[:, pl.ds(i * feat, feat)], part))
    copies = start_all(
        [pltpu.make_async_copy(a, b, sems.at[i]) for i, (a, b) in enumerate(pairs)]
    )

    earlier = (
        lax.broadcasted_iota(jnp.int32, (count, count), 0)
        < lax.broadcasted_iota(jnp.int32, (count, count), 1)
    ).astype(bf16)
    rows = -(-groups // 8) * 8
    line = lax.broadcasted_iota(jnp.int32, (rows, count), 0)
    slot = lax.broadcasted_iota(jnp.int32, (groups * room, count), 0)
    copies[0].wait()
    group = home_ref[...]
    if near:
        group = group ^ lax.axis_index("tile")
    member = jnp.where(group == line, 1.0, 0.0)
    rank = jnp.dot(member.astype(bf16), earlier, preferred_element_type=f32)
    rank = jnp.sum(rank * member, axis=0, keepdims=True).astype(jnp.int32)
    at = group * room + rank
    select16 = jnp.where(at == slot, 1.0, 0.0).astype(bf16)
    at_ref[...] = jnp.broadcast_to(at, at_ref.shape)
    copies[1].wait()
    bounds = jnp.concatenate(
        [boxes_ref[...], jnp.zeros((META - boxes_ref.shape[0], count), jnp.int32)], axis=0
    )
    bounds = lax.dot_general(
        bounds.astype(f32).astype(bf16),
        select16,
        (((1,), (1,)), ((), ())),
        preferred_element_type=f32,
    )
    copies[2].wait()
    placed = jnp.dot(select16, kernels_ref[...], preferred_element_type=f32)
    stride = block_refs[0].shape[0] * len(block_refs) // groups
    for g in range(groups):
        ref, at = (block_refs[g], 0) if len(block_refs) > 1 else (block_refs[0], g * stride)
        part = slice(g * room, (g + 1) * room)
        ref[at : at + stride, :] = jnp.concatenate(
            [
                placed[part],
                jnp.concatenate([bounds[:, part], jnp.zeros((META, feat - room), f32)], axis=1),
            ]
            + [jnp.zeros((stride - room - META, feat), f32)] * (stride > room + META),
            axis=0,
        ).astype(bf16)
    for copy in copies[3:]:
        copy.wait()


def pool_kernel(blocks, groups, room, *refs):
    block_refs, features_ref, out_refs = refs[:blocks][::-1], refs[blocks], refs[blocks + 1 :]
    bf16, f32 = jnp.bfloat16, jnp.float32
    slots, feat = groups * room, features_ref.shape[2]
    steps = features_ref.shape[0] // ROWS_PER_STEP
    stride = block_refs[0].shape[0] * blocks // groups
    unit = jnp.where(
        lax.broadcasted_iota(jnp.int32, (room, room), 0)
        == lax.broadcasted_iota(jnp.int32, (room, room), 1),
        1.0,
        0.0,
    ).astype(bf16)
    rows, bounds = [], []
    for g in range(groups):
        block = block_refs[g][...] if blocks > 1 else block_refs[0][g * stride : (g + 1) * stride, :]
        rows.append(block[:room].astype(f32))
        bounds.append(
            lax.dot_general(
                unit,
                block[room : room + META, :room],
                (((1,), (1,)), ((), ())),
                preferred_element_type=f32,
            )
        )
    rows16 = jnp.concatenate(rows, axis=0).astype(bf16)
    bounds = jnp.concatenate(bounds, axis=0)

    width = WC * TS
    tile_col = (lax.broadcasted_iota(jnp.int32, (slots, width), 1) // TS).astype(f32)
    column = (bounds[:, 2:3] <= tile_col) & (tile_col <= bounds[:, 3:4])
    inside = [
        jnp.where(column & (bounds[:, 0:1] <= r) & (r <= bounds[:, 1:2]), 1.0, 0.0)
        for r in range(SR)
    ]

    def cells(step):
        return features_ref[step * ROWS_PER_STEP : (step + 1) * ROWS_PER_STEP].reshape(
            ROWS_PER_STEP * width, feat
        )

    def logits(step):
        return lax.dot_general(
            rows16, cells(step), (((1,), (1,)), ((), ())), preferred_element_type=f32
        )

    pooled = jnp.zeros((slots, feat), f32)
    covered = jnp.zeros((slots, width), f32)
    now = logits(0)
    for step in range(steps):
        later = logits(step + 1) if step + 1 < steps else None
        mask = inside[step * ROWS_PER_STEP // TS]
        parts = []
        for j in range(ROWS_PER_STEP):
            part = mask * pl.reciprocal(
                1.0 + jnp.exp(-now[:, j * width : (j + 1) * width]), approx=True
            )
            covered = covered + part
            parts.append(part.astype(bf16))
        pooled = pooled + jnp.dot(
            jnp.concatenate(parts, axis=1), cells(step), preferred_element_type=f32
        )
        now = later
    area = jnp.sum(covered, axis=1, keepdims=True)
    ratio = pooled / area

    mean = jnp.mean(ratio, axis=1, keepdims=True)
    rounded = mean.astype(bf16).astype(f32)
    lane = lax.broadcasted_iota(jnp.int32, (slots, 128), 1)
    side = jnp.where(lane == 0, rounded, jnp.where(lane == 1, mean - rounded, 0.0)).T[:META]
    if feat > slots:
        side = jnp.concatenate([side, jnp.zeros((META, feat - slots), f32)], axis=1)
    owner = lax.broadcasted_iota(jnp.int32, (META, feat), 1) // room
    centred = ratio - mean
    for g in range(groups):
        ref, at = (out_refs[g], 0) if len(out_refs) > 1 else (out_refs[0], g * stride)
        ref[at : at + stride, :] = jnp.concatenate(
            [centred[g * room : (g + 1) * room], jnp.where(owner == g, side, 0.0)]
            + [jnp.zeros((stride - room - META, feat), f32)] * (stride > room + META),
            axis=0,
        ).astype(bf16)


def place_kernel(at_ref, pick_ref):
    count, slots = pick_ref.shape
    slot = lax.broadcasted_iota(jnp.int32, (slots, count), 0)
    pick_ref[...] = jnp.where(at_ref[:1, :] == slot, 1.0, 0.0).T.astype(pick_ref.dtype)


def through(normed, total, shard_refs):
    feat = total.shape[1]
    for ref in shard_refs:
        width = ref.shape[0] // 2
        for i in range(0, width, feat):
            hidden = jnp.dot(
                normed, ref[width + i : width + i + feat, :], preferred_element_type=jnp.float32
            )
            total = total + jnp.dot(
                jnp.maximum(hidden, 0.0).astype(normed.dtype),
                ref[i : i + feat, :],
                preferred_element_type=jnp.float32,
            )
    return total


def update_kernel(backs, shards, groups, room, *refs):
    back_refs, pick_ref, refs = refs[:backs], refs[backs], refs[backs + 1 :]
    (kernels_ref, gain_ref), shard_refs, refs = refs[:2], refs[2 : 2 + shards], refs[2 + shards :]
    normed_ref, total_ref = refs
    f32 = jnp.float32
    stride = back_refs[0].shape[0] * backs // groups
    blocks = [
        (ref[...] if backs > 1 else ref[i * stride : (i + 1) * stride, :]).astype(f32)
        for ref in back_refs[::-1]
        for i in range(groups // backs)
    ]
    pick = pick_ref[...]
    rows = jnp.concatenate([block[:room] for block in blocks], axis=0)
    side = sum(block[room : room + META, : groups * room] for block in blocks)
    means = lax.dot_general(
        pick, side.astype(pick.dtype), (((1,), (1,)), ((), ())), preferred_element_type=f32
    )
    ratio = jnp.dot(pick, rows.astype(pick.dtype), preferred_element_type=f32)
    ratio = ratio + (means[:, 0:1] + means[:, 1:2])
    merged = kernels_ref[...].astype(f32) + ratio
    centred = merged - jnp.mean(merged, axis=1, keepdims=True)
    spread = jnp.mean(centred * centred, axis=1, keepdims=True)
    normed = (centred * lax.rsqrt(spread + 1e-05) * gain_ref[...]).astype(normed_ref.dtype)
    normed_ref[...] = normed
    total_ref[...] = through(normed, merged, shard_refs)


def finish_kernel(normed_ref, total_ref, *refs):
    out_ref = refs[-1]
    out_ref[...] = through(normed_ref[...], total_ref[...], refs[:-1]).astype(out_ref.dtype)


def exchanged(x, axis, distance):
    return lax.ppermute(x, axis, [(i, i ^ distance) for i in range(lax.axis_size(axis))])


def all_exchanged(xs):
    strips, holders = lax.axis_size("tile"), lax.axis_size("inst")
    beside = 1 if holders % 2 == 0 else 0
    pairs = [(t, i) for t in range(strips) for i in range(holders)]
    return [
        lax.ppermute(
            xs[d],
            ("tile", "inst"),
            [(t * holders + i, (t ^ d) * holders + (i ^ beside)) for t, i in pairs],
        )
        for d in range(len(xs) - 1, 0, -1)
    ]


def local(features, kernels, home, boxes, gain, w_in, w_out):
    strips, holders = lax.axis_size("tile"), lax.axis_size("inst")
    count, feat = kernels.shape
    hidden = w_out.shape[0]
    most = min(count, max(2, 5 * count // (2 * strips)))
    room = -(-most // 8) * 8
    stride = -(-(room + META) // 16) * 16
    slots = strips * room
    near = strips & (strips - 1) == 0 and strips <= 8
    any_, hbm = pl.BlockSpec(memory_space=VMEM), pl.BlockSpec(memory_space=pltpu.HBM)

    parts = strips if near else 1
    *blocks, places, shard = pl.pallas_call(
        functools.partial(pack_kernel, near, strips, room),
        out_shape=[pltpu.VMEM((strips // parts * stride, feat), kernels.dtype)] * parts
        + [
            pltpu.VMEM((count, count), jnp.int32),
            pltpu.VMEM((2 * hidden, feat), w_out.dtype),
        ],
        in_specs=[hbm] * 5,
        out_specs=[any_] * (parts + 2),
        scratch_shapes=[
            pltpu.VMEM((1, count), home.dtype),
            pltpu.VMEM((boxes.shape[1], count), boxes.dtype),
            pltpu.VMEM((count, feat), kernels.dtype),
            pltpu.SemaphoreType.DMA((4 + hidden // feat,)),
        ],
        cost_estimate=pl.CostEstimate(
            flops=40 * slots * features.size, bytes_accessed=2 * features.size, transcendentals=0
        ),
        compiler_params=pltpu.CompilerParams(vmem_limit_bytes=24 << 20),
        name="pack",
    )(*[pltpu.with_memory_space_constraint(x, pltpu.HBM) for x in (home.T, boxes.T, kernels, w_out, w_in)])
    if near:
        blocks = all_exchanged(blocks) + [blocks[0]]
        outs = [jax.ShapeDtypeStruct((stride, feat), kernels.dtype)] * strips
    else:
        got = lax.all_to_all(
            blocks[0].reshape(strips, stride, feat), "tile", split_axis=0, concat_axis=0, tiled=True
        )
        blocks = [got.reshape(strips * stride, feat)]
        outs = [jax.ShapeDtypeStruct((strips * stride, feat), kernels.dtype)]

    shards = [shard]
    distance = holders // 2
    while distance > 1:
        shards += [exchanged(x, "inst", distance) for x in shards]
        distance //= 2

    back = pl.pallas_call(
        functools.partial(pool_kernel, len(blocks), strips, room),
        out_shape=outs,
        in_specs=[any_] * (len(blocks) + 1),
        out_specs=[any_] * len(outs),
        compiler_params=pltpu.CompilerParams(vmem_limit_bytes=24 << 20),
        cost_estimate=pl.CostEstimate(
            flops=40 * slots * features.size, bytes_accessed=2 * features.size, transcendentals=0
        ),
        name="pool",
    )(*blocks, features)
    if near:
        backs = all_exchanged(back) + [back[0]]
    else:
        got = lax.all_to_all(
            back[0].reshape(strips, stride, feat), "tile", split_axis=0, concat_axis=0, tiled=True
        )
        backs = [got.reshape(strips * stride, feat)]
    pick = pl.pallas_call(
        place_kernel,
        out_shape=pltpu.VMEM((count, slots), kernels.dtype),
        in_specs=[any_],
        out_specs=any_,
        compiler_params=pltpu.CompilerParams(vmem_limit_bytes=24 << 20),
        name="place",
    )(places)
    late = [exchanged(x, "inst", 1) for x in shards]
    shards.insert(1, late.pop(0))

    normed, total = pl.pallas_call(
        functools.partial(update_kernel, len(backs), len(shards), strips, room),
        out_shape=[
            jax.ShapeDtypeStruct((count, feat), kernels.dtype),
            jax.ShapeDtypeStruct((count, feat), jnp.float32),
        ],
        in_specs=[any_] * (len(backs) + 3 + len(shards)),
        out_specs=[any_] * 2,
        compiler_params=pltpu.CompilerParams(vmem_limit_bytes=24 << 20),
        cost_estimate=pl.CostEstimate(
            flops=40 * slots * features.size, bytes_accessed=2 * features.size, transcendentals=0
        ),
        name="update",
    )(*backs, pick, kernels, gain.reshape(1, feat), *shards)
    return pl.pallas_call(
        finish_kernel,
        out_shape=jax.ShapeDtypeStruct((count, feat), kernels.dtype),
        in_specs=[any_] * (2 + len(late)),
        out_specs=any_,
        compiler_params=pltpu.CompilerParams(vmem_limit_bytes=24 << 20),
        name="finish",
    )(normed, total, *late)


def solution(mesh):
    return jax.shard_map(
        local,
        mesh=mesh,
        in_specs=(
            P(("groups", "tile"), None, None),
            P(("groups", "tile", "inst"), None),
            P(("groups", "tile", "inst"), None),
            P(("groups", "tile", "inst"), None),
            P(),
            P(None, "inst"),
            P("inst", None),
        ),
        out_specs=P(("groups", "tile", "inst"), None),
        check_vma=False,
    )
```

```python
import functools

import jax
import jax.numpy as jnp
from jax import lax
from jax.experimental import pallas as pl
from jax.experimental.pallas import tpu as pltpu
from jax.sharding import PartitionSpec as P

TS = 32
SR = 2
WC = 8
META = 8
ROWS_PER_STEP = 2
VMEM = pltpu.VMEM


def start_all(copies):
    for copy in copies:
        copy.start()
    return copies


def pack_kernel(near, groups, room, *refs):
    home_hbm, boxes_hbm, kernels_hbm, w_out_hbm, w_in_hbm, block_refs = *refs[:5], refs[5:-6]
    at_ref, shard_ref, home_ref, boxes_ref, kernels_ref, sems = refs[-6:]
    bf16, f32 = jnp.bfloat16, jnp.float32
    count, feat = kernels_ref.shape
    hidden = w_out_hbm.shape[0]
    pairs = [(home_hbm, home_ref), (boxes_hbm, boxes_ref), (kernels_hbm, kernels_ref)]
    pairs.append((w_out_hbm, shard_ref.at[pl.ds(0, hidden)]))
    for i in range(hidden // feat):
        part = shard_ref.at[pl.ds(hidden + i * feat, feat)]
        pairs.append((w_in_hbm.at[:, pl.ds(i * feat, feat)], part))
    copies = start_all(
        [pltpu.make_async_copy(a, b, sems.at[i]) for i, (a, b) in enumerate(pairs)]
    )

    earlier = (
        lax.broadcasted_iota(jnp.int32, (count, count), 0)
        < lax.broadcasted_iota(jnp.int32, (count, count), 1)
    ).astype(bf16)
    rows = -(-groups // 8) * 8
    line = lax.broadcasted_iota(jnp.int32, (rows, count), 0)
    slot = lax.broadcasted_iota(jnp.int32, (groups * room, count), 0)
    copies[0].wait()
    group = home_ref[...]
    if near:
        group = group ^ lax.axis_index("tile")
    member = jnp.where(group == line, 1.0, 0.0)
    rank = jnp.dot(member.astype(bf16), earlier, preferred_element_type=f32)
    rank = jnp.sum(rank * member, axis=0, keepdims=True).astype(jnp.int32)
    at = group * room + rank
    select16 = jnp.where(at == slot, 1.0, 0.0).astype(bf16)
    at_ref[...] = jnp.broadcast_to(at, at_ref.shape)
    copies[1].wait()
    bounds = jnp.concatenate(
        [boxes_ref[...], jnp.zeros((META - boxes_ref.shape[0], count), jnp.int32)], axis=0
    )
    bounds = lax.dot_general(
        bounds.astype(f32).astype(bf16),
        select16,
        (((1,), (1,)), ((), ())),
        preferred_element_type=f32,
    )
    copies[2].wait()
    placed = jnp.dot(select16, kernels_ref[...], preferred_element_type=f32)
    stride = block_refs[0].shape[0] * len(block_refs) // groups
    for g in range(groups):
        ref, at = (block_refs[g], 0) if len(block_refs) > 1 else (block_refs[0], g * stride)
        part = slice(g * room, (g + 1) * room)
        ref[at : at + stride, :] = jnp.concatenate(
            [
                placed[part],
                jnp.concatenate([bounds[:, part], jnp.zeros((META, feat - room), f32)], axis=1),
            ]
            + [jnp.zeros((stride - room - META, feat), f32)] * (stride > room + META),
            axis=0,
        ).astype(bf16)
    for copy in copies[3:]:
        copy.wait()


def pool_kernel(blocks, groups, room, *refs):
    block_refs, features_ref, out_refs = refs[:blocks][::-1], refs[blocks], refs[blocks + 1 :]
    bf16, f32 = jnp.bfloat16, jnp.float32
    slots, feat = groups * room, features_ref.shape[2]
    steps = features_ref.shape[0] // ROWS_PER_STEP
    stride = block_refs[0].shape[0] * blocks // groups
    unit = jnp.where(
        lax.broadcasted_iota(jnp.int32, (room, room), 0)
        == lax.broadcasted_iota(jnp.int32, (room, room), 1),
        1.0,
        0.0,
    ).astype(bf16)
    rows, bounds = [], []
    for g in range(groups):
        block = block_refs[g][...] if blocks > 1 else block_refs[0][g * stride : (g + 1) * stride, :]
        rows.append(block[:room].astype(f32))
        bounds.append(
            lax.dot_general(
                unit,
                block[room : room + META, :room],
                (((1,), (1,)), ((), ())),
                preferred_element_type=f32,
            )
        )
    rows16 = jnp.concatenate(rows, axis=0).astype(bf16)
    bounds = jnp.concatenate(bounds, axis=0)

    width = WC * TS
    tile_col = (lax.broadcasted_iota(jnp.int32, (slots, width), 1) // TS).astype(f32)
    column = (bounds[:, 2:3] <= tile_col) & (tile_col <= bounds[:, 3:4])
    inside = [
        jnp.where(column & (bounds[:, 0:1] <= r) & (r <= bounds[:, 1:2]), 1.0, 0.0)
        for r in range(SR)
    ]

    def cells(step):
        return features_ref[step * ROWS_PER_STEP : (step + 1) * ROWS_PER_STEP].reshape(
            ROWS_PER_STEP * width, feat
        )

    def logits(step):
        return lax.dot_general(
            rows16, cells(step), (((1,), (1,)), ((), ())), preferred_element_type=f32
        )

    pooled = jnp.zeros((slots, feat), f32)
    covered = jnp.zeros((slots, width), f32)
    now = logits(0)
    for step in range(steps):
        later = logits(step + 1) if step + 1 < steps else None
        mask = inside[step * ROWS_PER_STEP // TS]
        parts = []
        for j in range(ROWS_PER_STEP):
            part = mask * pl.reciprocal(
                1.0 + jnp.exp(-now[:, j * width : (j + 1) * width]), approx=True
            )
            covered = covered + part
            parts.append(part.astype(bf16))
        pooled = pooled + jnp.dot(
            jnp.concatenate(parts, axis=1), cells(step), preferred_element_type=f32
        )
        now = later
    area = jnp.sum(covered, axis=1, keepdims=True)
    ratio = pooled / area

    mean = jnp.mean(ratio, axis=1, keepdims=True)
    rounded = mean.astype(bf16).astype(f32)
    lane = lax.broadcasted_iota(jnp.int32, (slots, 128), 1)
    side = jnp.where(lane == 0, rounded, jnp.where(lane == 1, mean - rounded, 0.0)).T[:META]
    if feat > slots:
        side = jnp.concatenate([side, jnp.zeros((META, feat - slots), f32)], axis=1)
    owner = lax.broadcasted_iota(jnp.int32, (META, feat), 1) // room
    centred = ratio - mean
    for g in range(groups):
        ref, at = (out_refs[g], 0) if len(out_refs) > 1 else (out_refs[0], g * stride)
        ref[at : at + stride, :] = jnp.concatenate(
            [centred[g * room : (g + 1) * room], jnp.where(owner == g, side, 0.0)]
            + [jnp.zeros((stride - room - META, feat), f32)] * (stride > room + META),
            axis=0,
        ).astype(bf16)


def place_kernel(at_ref, pick_ref):
    count, slots = pick_ref.shape
    slot = lax.broadcasted_iota(jnp.int32, (slots, count), 0)
    pick_ref[...] = jnp.where(at_ref[:1, :] == slot, 1.0, 0.0).T.astype(pick_ref.dtype)


def through(normed, total, shard_refs):
    feat = total.shape[1]
    for ref in shard_refs:
        width = ref.shape[0] // 2
        for i in range(0, width, feat):
            hidden = jnp.dot(
                normed, ref[width + i : width + i + feat, :], preferred_element_type=jnp.float32
            )
            total = total + jnp.dot(
                jnp.maximum(hidden, 0.0).astype(normed.dtype),
                ref[i : i + feat, :],
                preferred_element_type=jnp.float32,
            )
    return total


def update_kernel(backs, shards, groups, room, *refs):
    back_refs, pick_ref, refs = refs[:backs], refs[backs], refs[backs + 1 :]
    (kernels_ref, gain_ref), shard_refs, refs = refs[:2], refs[2 : 2 + shards], refs[2 + shards :]
    normed_ref, total_ref = refs
    f32 = jnp.float32
    stride = back_refs[0].shape[0] * backs // groups
    blocks = [
        (ref[...] if backs > 1 else ref[i * stride : (i + 1) * stride, :]).astype(f32)
        for ref in back_refs[::-1]
        for i in range(groups // backs)
    ]
    pick = pick_ref[...]
    rows = jnp.concatenate([block[:room] for block in blocks], axis=0)
    side = sum(block[room : room + META, : groups * room] for block in blocks)
    means = lax.dot_general(
        pick, side.astype(pick.dtype), (((1,), (1,)), ((), ())), preferred_element_type=f32
    )
    ratio = jnp.dot(pick, rows.astype(pick.dtype), preferred_element_type=f32)
    ratio = ratio + (means[:, 0:1] + means[:, 1:2])
    merged = kernels_ref[...].astype(f32) + ratio
    centred = merged - jnp.mean(merged, axis=1, keepdims=True)
    spread = jnp.mean(centred * centred, axis=1, keepdims=True)
    normed = (centred * lax.rsqrt(spread + 1e-05) * gain_ref[...]).astype(normed_ref.dtype)
    normed_ref[...] = normed
    total_ref[...] = through(normed, merged, shard_refs)


def finish_kernel(normed_ref, total_ref, *refs):
    out_ref = refs[-1]
    out_ref[...] = through(normed_ref[...], total_ref[...], refs[:-1]).astype(out_ref.dtype)


def exchanged(x, axis, distance):
    return lax.ppermute(x, axis, [(i, i ^ distance) for i in range(lax.axis_size(axis))])


def all_exchanged(xs):
    strips, holders = lax.axis_size("tile"), lax.axis_size("inst")
    beside = 1 if holders % 2 == 0 else 0
    pairs = [(t, i) for t in range(strips) for i in range(holders)]
    return [
        lax.ppermute(
            xs[d],
            ("tile", "inst"),
            [(t * holders + i, (t ^ d) * holders + (i ^ beside)) for t, i in pairs],
        )
        for d in range(len(xs) - 1, 0, -1)
    ]


def local(features, kernels, home, boxes, gain, w_in, w_out):
    strips, holders = lax.axis_size("tile"), lax.axis_size("inst")
    count, feat = kernels.shape
    hidden = w_out.shape[0]
    most = min(count, max(2, 5 * count // (2 * strips)))
    room = -(-most // 8) * 8
    stride = -(-(room + META) // 16) * 16
    slots = strips * room
    near = strips & (strips - 1) == 0 and strips <= 8
    any_, hbm = pl.BlockSpec(memory_space=VMEM), pl.BlockSpec(memory_space=pltpu.HBM)

    parts = strips if near else 1
    *blocks, places, shard = pl.pallas_call(
        functools.partial(pack_kernel, near, strips, room),
        out_shape=[pltpu.VMEM((strips // parts * stride, feat), kernels.dtype)] * parts
        + [
            pltpu.VMEM((count, count), jnp.int32),
            pltpu.VMEM((2 * hidden, feat), w_out.dtype),
        ],
        in_specs=[hbm] * 5,
        out_specs=[any_] * (parts + 2),
        scratch_shapes=[
            pltpu.VMEM((1, count), home.dtype),
            pltpu.VMEM((boxes.shape[1], count), boxes.dtype),
            pltpu.VMEM((count, feat), kernels.dtype),
            pltpu.SemaphoreType.DMA((4 + hidden // feat,)),
        ],
        cost_estimate=pl.CostEstimate(
            flops=40 * slots * features.size, bytes_accessed=2 * features.size, transcendentals=0
        ),
        compiler_params=pltpu.CompilerParams(vmem_limit_bytes=24 << 20),
        name="pack",
    )(*[pltpu.with_memory_space_constraint(x, pltpu.HBM) for x in (home.T, boxes.T, kernels, w_out, w_in)])
    if near:
        blocks = all_exchanged(blocks) + [blocks[0]]
        outs = [jax.ShapeDtypeStruct((stride, feat), kernels.dtype)] * strips
    else:
        got = lax.all_to_all(
            blocks[0].reshape(strips, stride, feat), "tile", split_axis=0, concat_axis=0, tiled=True
        )
        blocks = [got.reshape(strips * stride, feat)]
        outs = [jax.ShapeDtypeStruct((strips * stride, feat), kernels.dtype)]

    shards = [shard]
    distance = holders // 2
    while distance > 1:
        shards += [exchanged(x, "inst", distance) for x in shards]
        distance //= 2

    back = pl.pallas_call(
        functools.partial(pool_kernel, len(blocks), strips, room),
        out_shape=outs,
        in_specs=[any_] * (len(blocks) + 1),
        out_specs=[any_] * len(outs),
        compiler_params=pltpu.CompilerParams(vmem_limit_bytes=24 << 20),
        cost_estimate=pl.CostEstimate(
            flops=40 * slots * features.size, bytes_accessed=2 * features.size, transcendentals=0
        ),
        name="pool",
    )(*blocks, features)
    if near:
        backs = all_exchanged(back) + [back[0]]
    else:
        got = lax.all_to_all(
            back[0].reshape(strips, stride, feat), "tile", split_axis=0, concat_axis=0, tiled=True
        )
        backs = [got.reshape(strips * stride, feat)]
    pick = pl.pallas_call(
        place_kernel,
        out_shape=pltpu.VMEM((count, slots), kernels.dtype),
        in_specs=[any_],
        out_specs=any_,
        compiler_params=pltpu.CompilerParams(vmem_limit_bytes=24 << 20),
        name="place",
    )(places)
    late = [exchanged(x, "inst", 1) for x in shards]
    shards.insert(1, late.pop(0))

    normed, total = pl.pallas_call(
        functools.partial(update_kernel, len(backs), len(shards), strips, room),
        out_shape=[
            jax.ShapeDtypeStruct((count, feat), kernels.dtype),
            jax.ShapeDtypeStruct((count, feat), jnp.float32),
        ],
        in_specs=[any_] * (len(backs) + 3 + len(shards)),
        out_specs=[any_] * 2,
        compiler_params=pltpu.CompilerParams(vmem_limit_bytes=24 << 20),
        cost_estimate=pl.CostEstimate(
            flops=40 * slots * features.size, bytes_accessed=2 * features.size, transcendentals=0
        ),
        name="update",
    )(*backs, pick, kernels, gain.reshape(1, feat), *shards)
    return pl.pallas_call(
        finish_kernel,
        out_shape=jax.ShapeDtypeStruct((count, feat), kernels.dtype),
        in_specs=[any_] * (2 + len(late)),
        out_specs=any_,
        compiler_params=pltpu.CompilerParams(vmem_limit_bytes=24 << 20),
        name="finish",
    )(normed, total, *late)


def solution(mesh):
    return jax.shard_map(
        local,
        mesh=mesh,
        in_specs=(
            P(("groups", "tile"), None, None),
            P(("groups", "tile", "inst"), None),
            P(("groups", "tile", "inst"), None),
            P(("groups", "tile", "inst"), None),
            P(),
            P(None, "inst"),
            P("inst", None),
        ),
        out_specs=P(("groups", "tile", "inst"), None),
        check_vma=False,
    )
```
